128 devices in a mesh: slab: 4 (over x), box: 32 (over z, y, core).
Axes of the slice: x: 4, y: 4, z: 4, core: 2. Of those that a mesh axis runs over, the one named last changes fastest.
Arguments:
- sources: bfloat16 [4, 32, 512, 4096], P('slab', 'box'), may hold values from -6 to 6
- leaf_ops: bfloat16 [4, 32, 256, 4096], P('slab', 'box'), may hold values from -0.09375 to 0.09375
- edge_slot: int32 [4, 32, 256], P('slab', 'box'), may hold values from 0 to 255, each once within a row
- merge_ops: float32 [4, 32, 256, 256], P('slab', 'box'), may hold values from -0.25 to 0.25
- lift_ops: float32 [4, 32, 2048, 256], P('slab', 'box'), may hold values from -0.375 to 0.375
- coupling: float32 [4, 2048, 2048], P('slab', 'box'), may hold values from -0.0625 to 0.0625
- inverse: float32 [4, 2048, 2048], P('slab', 'box'), may hold values from -0.125 to 0.125
- boundary: float32 [512, 2048], P(None, 'box'), may hold values from -6 to 6
Outputs:
- interface_solution: float32 [4, 512, 2048], P('slab', None, 'box')
The draws below stay inside these ranges and needn't reach their ends.
Inputs may be any that keep to these rules, and one draw needn't show every extreme that they name: Each row edge_slot[s, b] holds every number from 0 to 255 once.
All inputs are finite; a program needn't handle non-finite values.
Results may differ from the reference program's by a relative error of at most 0.0003.
Values sent between devices are 32-bit elements; how exact they have to be, the bound alone decides.
No kernel may reach another device: no remote copies, remote signals or barrier semaphores. Data moves between devices by JAX's collectives and lax.ppermute only.
A program may use at most 64 MiB of HBM per device.

```python
import jax
import jax.numpy as jnp
from jax import lax

E = 256
P_SIZE = 4096
NI = 2048
R = 512
SLABS = 4
BOXES = 32
LEVELS = 5


def level_of(key, shape, shards, smallest, top_value):
    factor_of, own = 1.0, jax.random.fold_in(key, 6)
    for dim, parts in shards:
        steps = jnp.exp(jax.random.uniform(jax.random.fold_in(own, dim), (parts,), jnp.float32, smallest / len(shards), top_value / len(shards)))
        factor_of = factor_of * jnp.repeat(steps, shape[dim] // parts).reshape([-1 if axis == dim else 1 for axis in range(len(shape))])
    return factor_of


def centred(own_key, dims, width, reach, shards=(), held_as=jnp.bfloat16):
    factor_of = level_of(own_key, dims, shards, -0.22, 0.18) if shards else 1.0
    result = jax.random.normal(own_key, dims, jnp.float32) * width * factor_of
    return jnp.minimum(jnp.maximum(result, -reach), reach).astype(held_as)


def setup_inputs(seed: int = 0) -> dict:
    key_list = jax.random.split(jax.random.key(seed), 9)
    return {
        "sources": centred(key_list[0], (SLABS, BOXES, R, P_SIZE), 1.0, 6.0, ((0, 4), (1, 32))),
        "leaf_ops": centred(key_list[1], (SLABS, BOXES, E, P_SIZE), P_SIZE ** -0.5, 0.09375, ((0, 4), (1, 32))),
        "edge_slot": jax.vmap(lambda own: jax.random.permutation(own, E))(jax.random.split(key_list[2], SLABS * BOXES)).reshape((SLABS, BOXES, E)).astype(jnp.int32),
        "merge_ops": centred(key_list[3], (SLABS, BOXES, E, E), (2 * E) ** -0.5, 0.25, ((0, 4), (1, 32)), jnp.float32),
        "lift_ops": centred(key_list[4], (SLABS, BOXES, NI, E), E ** -0.5, 0.375, ((0, 4), (1, 32)), jnp.float32),
        "coupling": centred(key_list[5], (SLABS, NI, NI), (4 * NI) ** -0.5, 0.0625, ((0, 4), (1, 32)), jnp.float32),
        "inverse": centred(key_list[6], (SLABS, NI, NI), NI ** -0.5, 0.125, ((0, 4), (1, 32)), jnp.float32),
        "boundary": centred(key_list[7], (R, NI), 1.0, 6.0, ((1, 32),), jnp.float32),
    }


highest = lax.Precision.HIGHEST


def reorder(box_flux, slot_row):
    return jnp.take(box_flux, slot_row, axis=1)


def reference(sources, leaf_ops, edge_slot, merge_ops, lift_ops, coupling, inverse, boundary):
    previous = boundary
    outputs = []
    box_ids = jnp.arange(BOXES, dtype=jnp.int32)
    for slab_index in range(SLABS):
        box_flux = jnp.einsum("brp,bep->bre", sources[slab_index].astype(jnp.float32), leaf_ops[slab_index].astype(jnp.float32), precision=highest)
        current = jax.vmap(reorder)(box_flux, edge_slot[slab_index])
        for tree_level in range(LEVELS):
            bit_number = LEVELS - 1 - tree_level
            merged = jnp.einsum("bre,bfe->brf", current, merge_ops[slab_index], precision=highest)
            partner = jnp.bitwise_xor(box_ids, jnp.int32(2 ** bit_number))
            summed = merged + merged[partner]
            half_rows = summed.shape[1] // 2
            upper_half = jnp.bitwise_and(jnp.right_shift(box_ids, bit_number), 1)
            current = jnp.where((upper_half == 1)[:, None, None], summed[:, half_rows:], summed[:, :half_rows])
        lifted = jnp.einsum("bre,bie->bri", current, lift_ops[slab_index], precision=highest)
        slab_load = lifted.reshape(R, NI)
        corrected = slab_load - jnp.dot(previous, coupling[slab_index].T, precision=highest, preferred_element_type=jnp.float32)
        previous = jnp.dot(corrected, inverse[slab_index].T, precision=highest, preferred_element_type=jnp.float32)
        outputs.append(previous)
    return jnp.stack(outputs)
```

```python
import jax
import jax.numpy as jnp
from jax import lax
from jax.sharding import PartitionSpec as P

contract_last = (((1,), (1,)), ((), ()))
SIZES = (4, 4, 2)


def dot_t(a, b, precision=lax.Precision.HIGH):
    return lax.dot_general(a, b, contract_last, precision=precision, preferred_element_type=jnp.float32)


def split_box(b):
    return b // 8, (b // 2) % 4, b % 2


def join_box(z, y, c):
    return (z * 4 + y) * 2 + c


def rotate_z(value, by):
    pairs = []
    for b in range(32):
        z, y, c = split_box(b)
        pairs.append((b, join_box((z + by) % 4, y, c)))
    return lax.ppermute(value, "box", pairs)


def rotate_y(value, by):
    pairs = []
    for b in range(32):
        z, y, c = split_box(b)
        pairs.append((b, join_box(z, (y + by) % 4, c)))
    return lax.ppermute(value, "box", pairs)


def rotate_x(value, by):
    return lax.ppermute(value, "slab", [(i, (i + by) % 4) for i in range(4)])


def partner(value, bit):
    return lax.ppermute(value, "box", [(i, i ^ (1 << bit)) for i in range(32)])


def pick(stacked, index):
    return lax.dynamic_index_in_dim(stacked, index, 0, keepdims=False)


def in_order(from_behind, position):
    ring = [from_behind[0], from_behind[3], from_behind[2], from_behind[1]]
    return lax.dynamic_slice_in_dim(jnp.stack(ring + ring), (4 - position) % 4, 4, 0)


def exchange(pieces, position, rotate):
    own = pick(pieces, position)
    others = [rotate(pick(pieces, (position + k) % 4), k) for k in (1, 2, 3)]
    return in_order([own] + others, position)


def gather_sum(partial, rotate):
    return (partial + rotate(partial, 1)) + (rotate(partial, 2) + rotate(partial, 3))


def on_device(sources, leaf_ops, edge_slot, merge_ops, lift_ops, coupling, inverse, boundary):
    x = lax.axis_index("slab")
    box = lax.axis_index("box")
    z, y, c = box // 8, (box // 2) % 4, box % 2

    with jax.named_scope("operators"):
        c_pieces = coupling[0].reshape(64, 4, 512).transpose(1, 0, 2)
        c_block = exchange(c_pieces, z, rotate_z)
        i_pieces = inverse[0].reshape(64, 4, 4, 128).transpose(2, 0, 1, 3).reshape(4, 64, 512)
        i_block = exchange(i_pieces, y, rotate_y)

        def spread(block):
            mine = lax.all_gather(block.reshape(256, 512), "slab", axis=0)
            theirs = partner(mine, 0)
            low = jnp.where(c == 0, mine, theirs).reshape(4, 4, 1, 64, 512)
            high = jnp.where(c == 0, theirs, mine).reshape(4, 4, 1, 64, 512)
            return jnp.concatenate([low, high], axis=2).reshape(4, 512, 512)

        c_all = spread(c_block)
        i_all = spread(i_block)

    with jax.named_scope("boundary"):
        by_box = boundary.reshape(4, 4, 2, 16, 64)
        of_plane = lax.dynamic_index_in_dim(by_box, x, 1, keepdims=False)
        mine = lax.dynamic_index_in_dim(of_plane, c, 1, keepdims=False).reshape(64, 64)
        other = lax.dynamic_index_in_dim(of_plane, 1 - c, 1, keepdims=False).reshape(64, 64)
        theirs = partner(other, 0)
        wide = jnp.concatenate([jnp.where(c == 0, mine, theirs), jnp.where(c == 0, theirs, mine)], axis=1)
        rows = in_order([wide] + [rotate_y(wide, k) for k in (1, 2, 3)], y)
        entering = rows.transpose(1, 0, 2).reshape(64, 512)

    with jax.named_scope("reduction"):
        slot = edge_slot[0, 0]
        merge = merge_ops[0, 0]
        onehot = (slot[:, None] == jnp.arange(256, dtype=jnp.int32)[None, :]).astype(jnp.float32)
        merge_first = lax.dot_general(
            merge, onehot, (((1,), (0,)), ((), ())), precision=lax.Precision.HIGHEST,
            preferred_element_type=jnp.float32,
        )
        leaf = leaf_ops[0, 0]
        upper = (box >> 4) & 1
        given = lax.dynamic_slice_in_dim(sources[0, 0], (1 - upper) * 256, 256, 0)
        sent = partner(dot_t(dot_t(given, leaf, None), merge_first), 4)
        kept = lax.dynamic_slice_in_dim(sources[0, 0], upper * 256, 256, 0)
        current = dot_t(dot_t(kept, leaf, None), merge_first) + sent
        for bit in (3, 2, 1, 0):
            half = current.shape[0] // 2
            upper = (box >> bit) & 1
            given = lax.dynamic_slice_in_dim(current, (1 - upper) * half, half, 0)
            sent = partner(dot_t(given, merge), bit)
            kept = lax.dynamic_slice_in_dim(current, upper * half, half, 0)
            current = dot_t(kept, merge) + sent

    with jax.named_scope("loads"):
        lifted = dot_t(current, lift_ops[0, 0])
        l_pieces = lifted.reshape(16, 4, 4, 128).transpose(2, 0, 1, 3).reshape(4, 16, 512)
        arrived = []
        for k in range(4):
            pairs = []
            for s in range(4):
                for b in range(32):
                    bz, by, bc = split_box(b)
                    pairs.append((s * 32 + b, by * 32 + join_box(bz, (s + k) % 4, bc)))
            arrived.append(lax.ppermute(pick(l_pieces, (x + k) % 4), ("slab", "box"), pairs))
        loads = in_order(arrived, y)

    with jax.named_scope("chain"):
        solutions = []
        row0 = z * 16
        for s in range(4):
            partial = dot_t(-entering, c_all[s])
            own_rows = lax.dynamic_slice_in_dim(partial, row0, 16, 0) + loads[s]
            partial = lax.dynamic_update_slice_in_dim(partial, own_rows, row0, 0)
            corrected = gather_sum(partial, rotate_z)
            partial = dot_t(corrected, i_all[s])
            if s < 3:
                entering = gather_sum(partial, rotate_y)
                solutions.append(lax.dynamic_slice_in_dim(entering, y * 128, 128, 1))
            else:
                columns = partial.reshape(64, 4, 128).transpose(1, 0, 2)
                parts = [pick(columns, y)] + [rotate_y(pick(columns, (y + k) % 4), k) for k in (1, 2, 3)]
                solutions.append((parts[0] + parts[1]) + (parts[2] + parts[3]))

    with jax.named_scope("output"):
        by_plane = exchange(jnp.stack(solutions), x, rotate_x).reshape(4, 4, 16, 2, 64)
        mine = lax.dynamic_index_in_dim(by_plane, c, 3, keepdims=False)
        other = lax.dynamic_index_in_dim(by_plane, 1 - c, 3, keepdims=False)
        theirs = partner(other, 0)
        both = jnp.stack([jnp.where(c == 0, mine, theirs), jnp.where(c == 0, theirs, mine)])
        return both.transpose(2, 1, 0, 3, 4).reshape(1, 512, 64)


def solution(mesh):
    return jax.shard_map(
        on_device,
        mesh=mesh,
        in_specs=(
            P("slab", "box", None, None),
            P("slab", "box", None, None),
            P("slab", "box", None),
            P("slab", "box", None, None),
            P("slab", "box", None, None),
            P("slab", "box", None),
            P("slab", "box", None),
            P(None, "box"),
        ),
        out_specs=P("slab", None, "box"),
        check_vma=False,
    )
```

```python
import functools

import jax
import jax.numpy as jnp
from jax import lax
from jax.experimental import pallas as pl
from jax.experimental.pallas import tpu as pltpu
from jax.sharding import Mesh, PartitionSpec as P

contract_last = (((1,), (1,)), ((), ()))
f32 = jnp.float32


def dot_t(a, b, precision=lax.Precision.HIGH):
    return lax.dot_general(a, b, contract_last, precision=precision, preferred_element_type=f32)


def rotate(value, axis, by):
    return lax.ppermute(value, axis, [(i, (i + by) % 4) for i in range(4)])


def partner(value, axis, mask):
    count = 2 if axis == "c" else 4
    return lax.ppermute(value, axis, [(i, i ^ mask) for i in range(count)])


def select(choices, index):
    chosen = choices[0]
    for k in range(1, len(choices)):
        chosen = jnp.where(index == k, choices[k], chosen)
    return chosen


def local_kernel(body, out_shapes):
    return pl.pallas_call(
        body,
        out_shape=[jax.ShapeDtypeStruct(shape, f32) for shape in out_shapes],
        compiler_params=pltpu.CompilerParams(vmem_limit_bytes=16 * 2**20),
    )


def lanes(start, size):
    return pl.ds(pl.multiple_of(start, 128), size)


def rows(start, size):
    return pl.ds(pl.multiple_of(start, 16), size)


def cut_body(c_ref, i_ref, *outs):
    z, y, c = lax.axis_index("z"), lax.axis_index("y"), lax.axis_index("c")
    for k in range(4):
        to = lax.rem(2 * lax.rem(z, 2) + c + k, 4)
        outs[k][...] = c_ref[:, lanes(to * 512, 512)]
        to = lax.rem(2 * lax.rem(y, 2) + c + k, 4)
        for j in range(4):
            outs[4 + k][:, j * 128 : (j + 1) * 128] = i_ref[:, lanes(j * 512 + to * 128, 128)]


def stack_body(axis, a0, a1, a2, a3, out):
    position = lax.axis_index(axis)
    for k, part in enumerate((a0, a1, a2, a3)):
        out[rows(lax.rem(position + 4 - k, 4) * 64, 64), :] = part[...]


def widen_body(a0, a1, a2, a3, out):
    position = lax.axis_index("y")
    for k, part in enumerate((a0, a1, a2, a3)):
        out[:, lanes(lax.rem(position + 4 - k, 4) * 128, 128)] = part[...]


def finish_body(a0, a1, a2, a3, theirs, out):
    x, c = lax.axis_index("x"), lax.axis_index("c")
    for k, part in enumerate((a0, a1, a2, a3)):
        plane = lax.rem(x + 4 - k, 4)
        for z0 in range(4):
            mine = part[z0 * 16 : z0 * 16 + 16, :]
            other = theirs[k, z0 * 16 : z0 * 16 + 16, :]
            base = z0 * 128 + plane * 32
            out[0, rows(base + c * 16, 16), :] = jnp.where(c == 0, mine[:, :64], mine[:, 64:])
            out[0, rows(base + (1 - c) * 16, 16), :] = jnp.where(c == 0, other[:, :64], other[:, 64:])


def spread_rows(pieces, axis):
    arrived = []
    for k in range(4):
        pairs = []
        for i in range(4):
            for core in range(2):
                to = (2 * (i % 2) + core + k) % 4
                pairs.append((i * 2 + core, to * 2 + i // 2))
        arrived.append(lax.ppermute(pieces[k], (axis, "c"), pairs))
    block = local_kernel(functools.partial(stack_body, axis), [(256, 512)])(*arrived)[0]
    return lax.all_gather(block, ("x", "c"), axis=0).reshape(4, 512, 512)


def others(partial, axis):
    return [rotate(partial, axis, k) for k in (1, 2, 3)]


def add_up(parts):
    return (parts[0] + parts[1]) + (parts[2] + parts[3])


def on_device(sources, leaf_ops, edge_slot, merge_ops, lift_ops, coupling, inverse, boundary):
    x, z, y, c = (lax.axis_index(axis) for axis in ("x", "z", "y", "c"))

    with jax.named_scope("operators"):
        pieces = local_kernel(cut_body, [(64, 512)] * 8)(coupling[0], inverse[0])
        c_all = spread_rows(pieces[:4], "z")

    with jax.named_scope("reduction"):
        slot = edge_slot[0, 0]
        merge = merge_ops[0, 0]
        onehot = (slot[:, None] == jnp.arange(256, dtype=jnp.int32)[None, :]).astype(f32)
        merge_first = lax.dot_general(
            merge, onehot, (((1,), (0,)), ((), ())), precision=lax.Precision.HIGHEST, preferred_element_type=f32
        )
        leaf = leaf_ops[0, 0]
        bit = z >> 1
        next_bit = z & 1
        given = dot_t(lax.dynamic_slice_in_dim(sources[0, 0], (1 - bit) * 256, 256, 0), leaf, None)
        given_on = dot_t(lax.dynamic_slice_in_dim(given, (1 - next_bit) * 128, 128, 0), merge_first)
        given_kept = dot_t(lax.dynamic_slice_in_dim(given, next_bit * 128, 128, 0), merge_first)
        sent_on = partner(given_on, "z", 2)
        sent_kept = partner(given_kept, "z", 2)
        kept = dot_t(lax.dynamic_slice_in_dim(sources[0, 0], bit * 256, 256, 0), leaf, None)
        kept_on = dot_t(lax.dynamic_slice_in_dim(kept, (1 - next_bit) * 128, 128, 0), merge_first)
        kept_kept = dot_t(lax.dynamic_slice_in_dim(kept, next_bit * 128, 128, 0), merge_first)
        sent = partner(dot_t(kept_on + sent_on, merge), "z", 1)
        current = dot_t(kept_kept + sent_kept, merge) + sent
        for axis, mask, bit in (("y", 2, y >> 1), ("y", 1, y & 1), ("c", 1, c)):
            half = current.shape[0] // 2
            given = lax.dynamic_slice_in_dim(current, (1 - bit) * half, half, 0)
            sent = partner(dot_t(given, merge), axis, mask)
            kept = lax.dynamic_slice_in_dim(current, bit * half, half, 0)
            current = dot_t(kept, merge) + sent

    with jax.named_scope("operators"):
        late, _ = lax.optimization_barrier((pieces[4:], given_on))
        i_all = spread_rows(late, "y")

    with jax.named_scope("boundary"):
        by_box = boundary.reshape(4, 4, 2, 16, 64)
        of_plane = lax.dynamic_index_in_dim(by_box, x, 1, keepdims=False)
        mine = lax.dynamic_index_in_dim(of_plane, c, 1, keepdims=False).reshape(64, 64)
        other = lax.dynamic_index_in_dim(of_plane, 1 - c, 1, keepdims=False).reshape(64, 64)
        theirs = partner(other, "c", 1)
        wide = jnp.concatenate([jnp.where(c == 0, mine, theirs), jnp.where(c == 0, theirs, mine)], axis=1)
        entering = local_kernel(widen_body, [(64, 512)])(wide, *others(wide, "y"))[0]

    with jax.named_scope("loads"):
        lifted = dot_t(current, lift_ops[0, 0])
        l_pieces = [
            jnp.concatenate([lifted[:, j * 512 + i * 128 : j * 512 + (i + 1) * 128] for j in range(4)], axis=1)
            for i in range(4)
        ]
        arrived = []
        for k in range(4):
            pairs = [(s * 4 + y0, y0 * 4 + (s + k) % 4) for s in range(4) for y0 in range(4)]
            arrived.append(lax.ppermute(select(l_pieces, (x + k) % 4), ("x", "y"), pairs))
        own = (lax.broadcasted_iota(jnp.int32, (4, 16, 512), 0) == z)
        loads = []
        for s in range(4):
            of_slab = select(arrived, (y - s) % 4)
            loads.append(jnp.where(own, of_slab[None], 0.0).reshape(64, 512))

    with jax.named_scope("chain"):
        solutions = []
        for s in range(4):
            partial = loads[s] - dot_t(entering, c_all[s])
            corrected = add_up([partial] + others(partial, "z"))
            partial = dot_t(corrected, i_all[s])
            if s < 3:
                parts = [partial] + others(partial, "y")
                entering = add_up(parts)
                solutions.append(add_up([lax.dynamic_slice_in_dim(p, y * 128, 128, 1) for p in parts]))
            else:
                columns = [partial[:, i * 128 : (i + 1) * 128] for i in range(4)]
                parts = [select(columns, y)] + [rotate(select(columns, (y + k) % 4), "y", k) for k in (1, 2, 3)]
                solutions.append(add_up(parts))

    with jax.named_scope("output"):
        parts = [select(solutions, x)] + [rotate(select(solutions, (x + k) % 4), "x", k) for k in (1, 2, 3)]
        theirs = partner(jnp.stack(parts), "c", 1)
        return local_kernel(finish_body, [(1, 512, 64)])(*parts, theirs)[0]


def solution(mesh):
    wide = Mesh(mesh.devices.reshape(4, 4, 4, 2), ("x", "z", "y", "c"))
    box = ("z", "y", "c")
    return jax.shard_map(
        on_device,
        mesh=wide,
        in_specs=(
            P("x", box, None, None),
            P("x", box, None, None),
            P("x", box, None),
            P("x", box, None, None),
            P("x", box, None, None),
            P("x", box, None),
            P("x", box, None),
            P(None, box),
        ),
        out_specs=P("x", None, box),
        check_vma=False,
    )
```

```python
import functools

import jax
import jax.numpy as jnp
from jax import lax
from jax.experimental import pallas as pl
from jax.experimental.pallas import tpu as pltpu
from jax.sharding import Mesh, PartitionSpec as P

contract_last = (((1,), (1,)), ((), ()))
f32 = jnp.float32
bf16 = jnp.bfloat16


def dot_t(a, b, precision=lax.Precision.HIGH):
    return lax.dot_general(a, b, contract_last, precision=precision, preferred_element_type=f32)


def swap(value, axis, mask):
    count = 2 if axis == "c" else 4
    return lax.ppermute(value, axis, [(i, i ^ mask) for i in range(count)])


def select(choices, index):
    chosen = choices[0]
    for k in range(1, len(choices)):
        chosen = jnp.where(index == k, choices[k], chosen)
    return chosen


def local_kernel(body, out_shapes, flops=0, bytes_accessed=2**20, scratch=()):
    return pl.pallas_call(
        body,
        out_shape=[jax.ShapeDtypeStruct(shape, f32) for shape in out_shapes],
        scratch_shapes=[pltpu.VMEM(shape, f32) for shape in scratch],
        cost_estimate=pl.CostEstimate(flops=flops, bytes_accessed=bytes_accessed, transcendentals=0),
        compiler_params=pltpu.CompilerParams(vmem_limit_bytes=16 * 2**20),
    )


def lanes(start, size=128):
    return pl.ds(pl.multiple_of(start, 128), size)


def rows(start, size):
    return pl.ds(pl.multiple_of(start, 16), size)


def cut_body(c_ref, i_ref, *outs):
    z, y = lax.axis_index("z"), lax.axis_index("y")
    for k in range(4):
        for j in range(4):
            for out, part in (
                (outs[k], c_ref[:, lanes((z ^ k) * 512 + j * 128)]),
                (outs[4 + k], i_ref[:, lanes(j * 512 + (y ^ k) * 128)]),
            ):
                out[:, j * 64 : j * 64 + 64] = part[:, :64]
                out[:, 256 + j * 64 : 256 + j * 64 + 64] = part[:, 64:]


def stack_body(*refs):
    z, y = lax.axis_index("z"), lax.axis_index("y")
    out = refs[8]
    for k in range(4):
        out[0, rows((z ^ k) * 64, 64), :] = refs[k][...]
        out[1, rows((y ^ k) * 64, 64), :] = refs[4 + k][...]


def widen_body(a0, a1, a2, a3, out, scratch):
    y = lax.axis_index("y")
    for k, part in enumerate((a0, a1, a2, a3)):
        scratch[y ^ k] = part[...]
    for j in range(4):
        part = scratch[j]
        out[:, j * 64 : j * 64 + 64] = part[:, :64]
        out[:, 256 + j * 64 : 256 + j * 64 + 64] = part[:, 64:]


def split(value):
    high = value.astype(bf16)
    return high, (value - high.astype(f32)).astype(bf16)


def product(value, operator):
    def dot(a, b):
        return lax.dot_general(a, b, contract_last, preferred_element_type=f32)

    vh, vl = split(value)
    oh, ol = split(operator)
    return dot(vh, oh) + (dot(vh, ol) + dot(vl, oh))


def natural_columns(ref, y):
    parts = []
    for core in range(2):
        wide = ref[:, lanes(core * 256 + lax.shift_right_logical(y, 1) * 128)]
        parts.append(jnp.where((y & 1) == 0, wide[:, :64], wide[:, 64:]))
    return jnp.concatenate(parts, axis=1)


def add_up(refs):
    total = refs[0][...]
    for ref in refs[1:]:
        total = total + ref[...]
    return total


def couple_body(n_parts, *refs):
    parts, (load, w0, w1), outs = refs[:n_parts], refs[n_parts : n_parts + 3], refs[n_parts + 3 :]
    out = outs[0]
    entering = add_up(parts)
    if n_parts > 1:
        total = outs[2]
        total[...] = entering
        outs[1][...] = natural_columns(total, lax.axis_index("y"))
    out[:, :256] = -product(entering, w0[...])
    out[:, 256:] = -product(entering, w1[...])
    own = rows(lax.axis_index("z") * 16, 16)
    out[own, :] = out[own, :] + load[...]


def invert_body(last, a0, a1, a2, a3, w0, w1, out, *pieces):
    corrected = add_up((a0, a1, a2, a3))
    out[:, :256] = product(corrected, w0[...])
    out[:, 256:] = product(corrected, w1[...])
    if last:
        y = lax.axis_index("y")
        for k, piece in enumerate(pieces):
            piece[...] = natural_columns(out, y ^ k)


def finish_body(a0, a1, a2, a3, theirs, out):
    x, c = lax.axis_index("x"), lax.axis_index("c")
    for k, part in enumerate((a0, a1, a2, a3)):
        for z0 in range(4):
            mine = part[z0 * 16 : z0 * 16 + 16, :]
            other = theirs[k, z0 * 16 : z0 * 16 + 16, :]
            base = z0 * 128 + (x ^ k) * 32
            out[0, rows(base + c * 16, 16), :] = jnp.where(c == 0, mine[:, :64], mine[:, 64:])
            out[0, rows(base + (1 - c) * 16, 16), :] = jnp.where(c == 0, other[:, :64], other[:, 64:])


def on_device(sources, leaf_ops, edge_slot, merge_ops, lift_ops, coupling, inverse, boundary):
    x, z, y, c = (lax.axis_index(axis) for axis in ("x", "z", "y", "c"))

    with jax.named_scope("boundary"):
        by_box = boundary.reshape(4, 4, 2, 16, 64)
        of_plane = lax.dynamic_index_in_dim(by_box, x, 1, keepdims=False)
        mine = lax.dynamic_index_in_dim(of_plane, c, 1, keepdims=False).reshape(64, 64)
        other = lax.dynamic_index_in_dim(of_plane, 1 - c, 1, keepdims=False).reshape(64, 64)
        theirs = swap(other, "c", 1)
        wide = jnp.concatenate([jnp.where(c == 0, mine, theirs), jnp.where(c == 0, theirs, mine)], axis=1)

    with jax.named_scope("operators"):
        pieces = local_kernel(cut_body, [(64, 512)] * 8)(coupling[0], inverse[0])
        arrived = (
            [pieces[0]]
            + [swap(pieces[k], "z", k) for k in (1, 2, 3)]
            + [pieces[4]]
            + [swap(pieces[4 + k], "y", k) for k in (1, 2, 3)]
        )
        block = local_kernel(stack_body, [(2, 256, 512)])(*arrived)[0]
        operators = lax.all_gather(block, ("x", "c"), axis=0)

    with jax.named_scope("reduction"):
        slot = edge_slot[0, 0]
        merge = merge_ops[0, 0]
        onehot = (slot[:, None] == jnp.arange(256, dtype=jnp.int32)[None, :]).astype(f32)
        merge_first = lax.dot_general(
            merge, onehot, (((1,), (0,)), ((), ())), precision=lax.Precision.HIGHEST, preferred_element_type=f32
        )
        leaf = leaf_ops[0, 0]
        bit = z >> 1
        next_bit = z & 1
        given = dot_t(lax.dynamic_slice_in_dim(sources[0, 0], (1 - bit) * 256, 256, 0), leaf, None)
        given_on = dot_t(lax.dynamic_slice_in_dim(given, (1 - next_bit) * 128, 128, 0), merge_first)
        given_kept = dot_t(lax.dynamic_slice_in_dim(given, next_bit * 128, 128, 0), merge_first)
        given_on, wide = lax.optimization_barrier((given_on, wide))
        sent_on = swap(given_on, "z", 2)
        sent_kept = swap(given_kept, "z", 2)
        entering_parts = [wide] + [swap(wide, "y", k) for k in (1, 2, 3)]
        kept = dot_t(lax.dynamic_slice_in_dim(sources[0, 0], bit * 256, 256, 0), leaf, None)
        kept_on = dot_t(lax.dynamic_slice_in_dim(kept, (1 - next_bit) * 128, 128, 0), merge_first)
        kept_kept = dot_t(lax.dynamic_slice_in_dim(kept, next_bit * 128, 128, 0), merge_first)
        sent = swap(dot_t(kept_on + sent_on, merge), "z", 1)
        current = dot_t(kept_kept + sent_kept, merge) + sent
        entering = local_kernel(widen_body, [(64, 512)], scratch=[(4, 64, 128)])(*entering_parts)[0]
        current, entering = lax.optimization_barrier((current, entering))
        for axis, mask, bit in (("y", 2, y >> 1), ("y", 1, y & 1), ("c", 1, c)):
            half = current.shape[0] // 2
            given = lax.dynamic_slice_in_dim(current, (1 - bit) * half, half, 0)
            sent = swap(dot_t(given, merge), axis, mask)
            kept = lax.dynamic_slice_in_dim(current, bit * half, half, 0)
            current = dot_t(kept, merge) + sent

    with jax.named_scope("loads"):
        lift = lift_ops[0, 0].reshape(4, 4, 2, 64, 256).transpose(1, 2, 0, 3, 4).reshape(2048, 256)
        lifted = dot_t(current, lift)
        l_pieces = [lifted[:, i * 512 : (i + 1) * 512] for i in range(4)]
        arrived = []
        for k in range(4):
            pairs = [(s * 4 + y0, y0 * 4 + (s + k) % 4) for s in range(4) for y0 in range(4)]
            arrived.append(lax.ppermute(select(l_pieces, (x + k) % 4), ("x", "y"), pairs))
        loads = [select(arrived, (y - s) % 4) for s in range(4)]

    with jax.named_scope("chain"):
        solutions = []
        flops = 3 * 2 * 64 * 512 * 512
        parts = [entering]
        for s in range(4):
            out_shapes = [(64, 512)] + ([(64, 128)] if s else [])
            couple = local_kernel(
                functools.partial(couple_body, len(parts)), out_shapes, flops, 2**21, [(64, 512)] if s else []
            )
            results = couple(*parts, loads[s], operators[2 * s, 0], operators[2 * s + 1, 0])
            solutions += results[1:]
            partial = results[0]
            parts = [partial] + [swap(partial, "z", k) for k in (1, 2, 3)]
            invert = local_kernel(
                functools.partial(invert_body, s == 3),
                [(64, 512)] + ([(64, 128)] * 4 if s == 3 else []),
                flops,
                2**21,
            )
            results = invert(*parts, operators[2 * s, 1], operators[2 * s + 1, 1])
            partial = results[0]
            if s < 3:
                parts = [partial] + [swap(partial, "y", k) for k in (1, 2, 3)]
            else:
                parts = [results[1]] + [swap(results[1 + k], "y", k) for k in (1, 2, 3)]
                solutions.append((parts[0] + parts[1]) + (parts[2] + parts[3]))

    with jax.named_scope("output"):
        parts = [select(solutions, x)] + [swap(select(solutions, x ^ k), "x", k) for k in (1, 2, 3)]
        theirs = swap(jnp.stack(parts), "c", 1)
        return local_kernel(finish_body, [(1, 512, 64)])(*parts, theirs)[0]


def solution(mesh):
    wide = Mesh(mesh.devices.reshape(4, 4, 4, 2), ("x", "z", "y", "c"))
    box = ("z", "y", "c")
    return jax.shard_map(
        on_device,
        mesh=wide,
        in_specs=(
            P("x", box, None, None),
            P("x", box, None, None),
            P("x", box, None),
            P("x", box, None, None),
            P("x", box, None, None),
            P("x", box, None),
            P("x", box, None),
            P(None, box),
        ),
        out_specs=P("x", None, box),
        check_vma=False,
    )
```

```python
import functools

import jax
import jax.numpy as jnp
from jax import lax
from jax.experimental import pallas as pl
from jax.experimental.pallas import tpu as pltpu
from jax.sharding import Mesh, PartitionSpec as P

contract_last = (((1,), (1,)), ((), ()))
f32 = jnp.float32
bf16 = jnp.bfloat16


def dot_t(a, b, precision=lax.Precision.HIGH):
    return lax.dot_general(a, b, contract_last, precision=precision, preferred_element_type=f32)


def swap(value, axis, mask):
    count = 2 if axis == "c" else 4
    return lax.ppermute(value, axis, [(i, i ^ mask) for i in range(count)])


def select(choices, index):
    chosen = choices[0]
    for k in range(1, len(choices)):
        chosen = jnp.where(index == k, choices[k], chosen)
    return chosen


def local_kernel(body, out_shapes, flops=0, bytes_accessed=2**20, scratch=()):
    return pl.pallas_call(
        body,
        out_shape=[jax.ShapeDtypeStruct(shape, f32) for shape in out_shapes],
        scratch_shapes=[pltpu.VMEM(shape, f32) for shape in scratch],
        cost_estimate=pl.CostEstimate(flops=flops, bytes_accessed=bytes_accessed, transcendentals=0),
        compiler_params=pltpu.CompilerParams(vmem_limit_bytes=16 * 2**20),
    )


def lanes(start, size=128):
    return pl.ds(pl.multiple_of(start, 128), size)


def rows(start, size):
    return pl.ds(pl.multiple_of(start, 16), size)


def cut_body(by_z, ref, *outs):
    position = lax.axis_index("z" if by_z else "y")
    for k, out in enumerate(outs):
        for j in range(4):
            start = (position ^ k) * 512 + j * 128 if by_z else j * 512 + (position ^ k) * 128
            part = ref[:, lanes(start)]
            out[:, j * 64 : j * 64 + 64] = part[:, :64]
            out[:, 256 + j * 64 : 256 + j * 64 + 64] = part[:, 64:]


def stack_body(axis, a0, a1, a2, a3, out):
    position = lax.axis_index(axis)
    for k, part in enumerate((a0, a1, a2, a3)):
        out[rows((position ^ k) * 64, 64), :] = part[...]


def arrange_body(*refs):
    own, theirs, outs, sems = refs[:4], refs[4:8], refs[8:16], refs[16]
    x, c = lax.axis_index("x"), lax.axis_index("c")
    for s in range(4):
        for k in range(4):
            for core in range(2):
                mine, other = (own[k], theirs[k]) if core == 0 else (theirs[k], own[k])

                @pl.when(jnp.logical_and((x ^ k) == s, c == core))
                def _():
                    pltpu.make_async_copy(mine, outs[2 * s], sems.at[2 * s]).start()
                    pltpu.make_async_copy(other, outs[2 * s + 1], sems.at[2 * s + 1]).start()

    for i in range(8):
        pltpu.make_async_copy(own[0], outs[i], sems.at[i]).wait()


def lift_body(current, lift, *refs):
    outs, lifted = refs[:4], refs[4]
    x = lax.axis_index("x")
    for j in range(4):
        lifted[:, j * 512 : (j + 1) * 512] = product(current[...], lift[j * 512 : (j + 1) * 512, :])
    for k, out in enumerate(outs):
        to = lax.rem(x + k, 4)
        for j in range(4):
            part = lifted[:, lanes(j * 512 + to * 128)]
            out[:, j * 64 : j * 64 + 64] = part[:, :64]
            out[:, 256 + j * 64 : 256 + j * 64 + 64] = part[:, 64:]


def widen_body(a0, a1, a2, a3, out, scratch):
    y = lax.axis_index("y")
    for k, part in enumerate((a0, a1, a2, a3)):
        scratch[y ^ k] = part[...]
    for j in range(4):
        part = scratch[j]
        out[:, j * 64 : j * 64 + 64] = part[:, :64]
        out[:, 256 + j * 64 : 256 + j * 64 + 64] = part[:, 64:]


def split(value):
    high = value.astype(bf16)
    return high, (value - high.astype(f32)).astype(bf16)


def product(value, operator):
    def dot(a, b):
        return lax.dot_general(a, b, contract_last, preferred_element_type=f32)

    vh, vl = split(value)
    oh, ol = split(operator)
    return dot(vh, oh) + (dot(vh, ol) + dot(vl, oh))


def natural_columns(ref, y):
    parts = []
    for core in range(2):
        wide = ref[:, lanes(core * 256 + lax.shift_right_logical(y, 1) * 128)]
        parts.append(jnp.where((y & 1) == 0, wide[:, :64], wide[:, 64:]))
    return jnp.concatenate(parts, axis=1)


def add_up(refs):
    total = refs[0][...]
    for ref in refs[1:]:
        total = total + ref[...]
    return total


def couple_body(n_parts, *refs):
    parts, (load, w0, w1), outs = refs[:n_parts], refs[n_parts : n_parts + 3], refs[n_parts + 3 :]
    out = outs[0]
    entering = add_up(parts)
    if n_parts > 1:
        total = outs[2]
        total[...] = entering
        outs[1][...] = natural_columns(total, lax.axis_index("y"))
    out[:, :256] = -product(entering, w0[...])
    out[:, 256:] = -product(entering, w1[...])
    own = rows(lax.axis_index("z") * 16, 16)
    out[own, :] = out[own, :] + load[...]


def invert_body(last, a0, a1, a2, a3, w0, w1, out, *pieces):
    corrected = add_up((a0, a1, a2, a3))
    out[:, :256] = product(corrected, w0[...])
    out[:, 256:] = product(corrected, w1[...])
    if last:
        y = lax.axis_index("y")
        for k, piece in enumerate(pieces):
            piece[...] = natural_columns(out, y ^ k)


def finish_body(a0, a1, a2, a3, theirs, out):
    x, c = lax.axis_index("x"), lax.axis_index("c")
    for k, part in enumerate((a0, a1, a2, a3)):
        for z0 in range(4):
            mine = part[z0 * 16 : z0 * 16 + 16, :]
            other = theirs[k, z0 * 16 : z0 * 16 + 16, :]
            base = z0 * 128 + (x ^ k) * 32
            out[0, rows(base + c * 16, 16), :] = jnp.where(c == 0, mine[:, :64], mine[:, 64:])
            out[0, rows(base + (1 - c) * 16, 16), :] = jnp.where(c == 0, other[:, :64], other[:, 64:])


def after(values, done):
    return lax.optimization_barrier((values, done))[0]


def on_device(sources, leaf_ops, edge_slot, merge_ops, lift_ops, coupling, inverse, boundary):
    x, z, y, c = (lax.axis_index(axis) for axis in ("x", "z", "y", "c"))
    slot = edge_slot[0, 0]
    merge = merge_ops[0, 0]
    leaf = leaf_ops[0, 0]

    def part_of(value, bit, size):
        given = lax.dynamic_slice_in_dim(value, (1 - bit) * size, size, 0)
        return given, lax.dynamic_slice_in_dim(value, bit * size, size, 0)

    with jax.named_scope("reduction"):
        onehot = (slot[:, None] == jnp.arange(256, dtype=jnp.int32)[None, :]).astype(f32)
        merge_first = lax.dot_general(
            merge, onehot, (((1,), (0,)), ((), ())), precision=lax.Precision.HIGHEST, preferred_element_type=f32
        )
        given, kept = part_of(sources[0, 0], z >> 1, 256)
        given_on, given_kept = part_of(dot_t(given, leaf, None), z & 1, 128)
        given_on = dot_t(given_on, merge_first)
        sent_on = swap(given_on, "z", 2)
        sent_kept = swap(dot_t(given_kept, merge_first), "z", 2)
        kept_on, kept_kept = part_of(dot_t(kept, leaf, None), z & 1, 128)
        kept_on = dot_t(kept_on, merge_first) + sent_on
        kept_kept = dot_t(kept_kept, merge_first) + sent_kept

    with jax.named_scope("operators"):
        c_pieces = after(local_kernel(functools.partial(cut_body, True), [(64, 512)] * 4)(coupling[0]), given_on)
        c_parts = [c_pieces[0]] + [swap(c_pieces[k], "z", k) for k in (1, 2, 3)]
        c_parts = after(c_parts, kept_on)
        c_block = local_kernel(functools.partial(stack_body, "z"), [(256, 512)])(*c_parts)[0]
        c_all = lax.all_gather(c_block, ("x", "c"), axis=0)

        i_pieces = after(local_kernel(functools.partial(cut_body, False), [(64, 512)] * 4)(inverse[0]), kept_on)
        i_parts = [i_pieces[0]] + [swap(i_pieces[k], "y", k) for k in (1, 2, 3)]

    with jax.named_scope("reduction"):
        level1 = dot_t(kept_kept, merge) + swap(dot_t(kept_on, merge), "z", 1)

    with jax.named_scope("operators"):
        i_parts = after(i_parts, level1)
        i_block = local_kernel(functools.partial(stack_body, "y"), [(256, 512)])(*i_parts)[0]
        i_own = [i_block] + [swap(i_block, "x", k) for k in (2, 1, 3)]
        i_own = [i_own[0], i_own[2], i_own[1], i_own[3]]
        i_theirs = [swap(block, "c", 1) for block in i_own]

    with jax.named_scope("boundary"):
        by_box = after(boundary, level1).reshape(4, 4, 2, 16, 64)
        of_plane = lax.dynamic_index_in_dim(by_box, x, 1, keepdims=False)
        mine = lax.dynamic_index_in_dim(of_plane, c, 1, keepdims=False).reshape(64, 64)
        other = lax.dynamic_index_in_dim(of_plane, 1 - c, 1, keepdims=False).reshape(64, 64)
        theirs = swap(other, "c", 1)
        wide = jnp.concatenate([jnp.where(c == 0, mine, theirs), jnp.where(c == 0, theirs, mine)], axis=1)

    with jax.named_scope("reduction"):
        given, kept = part_of(level1, y >> 1, 64)
        level2 = dot_t(kept, merge) + swap(dot_t(given, merge), "y", 2)

    with jax.named_scope("boundary"):
        wide = after(wide, level2)
        entering_parts = [wide] + [swap(wide, "y", k) for k in (1, 2, 3)]

    with jax.named_scope("reduction"):
        given, kept = part_of(level2, y & 1, 32)
        level3 = dot_t(kept, merge) + swap(dot_t(given, merge), "y", 1)
        given, kept = part_of(level3, c, 16)
        current = dot_t(kept, merge) + swap(dot_t(given, merge), "c", 1)

    with jax.named_scope("boundary"):
        entering_parts = after(entering_parts, level3)
        entering = local_kernel(widen_body, [(64, 512)], scratch=[(4, 64, 128)])(*entering_parts)[0]

    with jax.named_scope("loads"):
        l_pieces = local_kernel(lift_body, [(16, 512)] * 4, 3 * 2 * 16 * 256 * 2048, 2**21, [(16, 2048)])(
            current, lift_ops[0, 0]
        )
        arrived = []
        for k in range(4):
            pairs = [(s * 4 + y0, y0 * 4 + (s + k) % 4) for s in range(4) for y0 in range(4)]
            arrived.append(lax.ppermute(l_pieces[k], ("x", "y"), pairs))
        loads = [select(arrived, (y - s) % 4) for s in range(4)]

    with jax.named_scope("chain"):
        solutions = []
        flops = 3 * 2 * 64 * 512 * 512
        parts = [entering]
        for s in range(4):
            out_shapes = [(64, 512)] + ([(64, 128)] if s else [])
            couple = local_kernel(
                functools.partial(couple_body, len(parts)), out_shapes, flops, 2**21, [(64, 512)] if s else []
            )
            of_slab = after(c_all, partial) if s else c_all
            results = couple(*parts, loads[s], of_slab[2 * s], of_slab[2 * s + 1])
            solutions += results[1:]
            partial = results[0]
            parts = [partial] + [swap(partial, "z", k) for k in (1, 2, 3)]
            if s == 0:
                i_all = pl.pallas_call(
                    arrange_body,
                    out_shape=[jax.ShapeDtypeStruct((256, 512), f32)] * 8,
                    in_specs=[pl.BlockSpec(memory_space=pl.ANY)] * 8,
                    out_specs=[pl.BlockSpec(memory_space=pltpu.VMEM)] * 8,
                    scratch_shapes=[pltpu.SemaphoreType.DMA((8,))],
                    cost_estimate=pl.CostEstimate(flops=0, bytes_accessed=2**23, transcendentals=0),
                    compiler_params=pltpu.CompilerParams(vmem_limit_bytes=16 * 2**20),
                )(*after(i_own, partial), *i_theirs)
            invert = local_kernel(
                functools.partial(invert_body, s == 3),
                [(64, 512)] + ([(64, 128)] * 4 if s == 3 else []),
                flops,
                2**21,
            )
            results = invert(*parts, i_all[2 * s], i_all[2 * s + 1])
            partial = results[0]
            if s < 3:
                parts = [partial] + [swap(partial, "y", k) for k in (1, 2, 3)]
            else:
                parts = [results[1]] + [swap(results[1 + k], "y", k) for k in (1, 2, 3)]
                solutions.append((parts[0] + parts[1]) + (parts[2] + parts[3]))

    with jax.named_scope("output"):
        parts = [select(solutions, x)] + [swap(select(solutions, x ^ k), "x", k) for k in (1, 2, 3)]
        theirs = swap(jnp.stack(parts), "c", 1)
        return local_kernel(finish_body, [(1, 512, 64)])(*parts, theirs)[0]


def solution(mesh):
    wide = Mesh(mesh.devices.reshape(4, 4, 4, 2), ("x", "z", "y", "c"))
    box = ("z", "y", "c")
    return jax.shard_map(
        on_device,
        mesh=wide,
        in_specs=(
            P("x", box, None, None),
            P("x", box, None, None),
            P("x", box, None),
            P("x", box, None, None),
            P("x", box, None, None),
            P("x", box, None),
            P("x", box, None),
            P(None, box),
        ),
        out_specs=P("x", None, box),
        check_vma=False,
    )
```

```python
import functools

import jax
import jax.numpy as jnp
from jax import lax
from jax.experimental import pallas as pl
from jax.experimental.pallas import tpu as pltpu
from jax.sharding import Mesh, PartitionSpec as P

contract_last = (((1,), (1,)), ((), ()))
f32 = jnp.float32
bf16 = jnp.bfloat16


def dot_t(a, b, precision=lax.Precision.HIGH):
    return lax.dot_general(a, b, contract_last, precision=precision, preferred_element_type=f32)


def swap(value, axis, mask):
    count = 2 if axis == "c" else 4
    return lax.ppermute(value, axis, [(i, i ^ mask) for i in range(count)])


def select(choices, index):
    chosen = choices[0]
    for k in range(1, len(choices)):
        chosen = jnp.where(index == k, choices[k], chosen)
    return chosen


def local_kernel(body, out_shapes, flops=0, bytes_accessed=2**20, scratch=()):
    return pl.pallas_call(
        body,
        out_shape=[jax.ShapeDtypeStruct(shape, f32) for shape in out_shapes],
        scratch_shapes=[pltpu.VMEM(shape, f32) for shape in scratch],
        cost_estimate=pl.CostEstimate(flops=flops, bytes_accessed=bytes_accessed, transcendentals=0),
        compiler_params=pltpu.CompilerParams(vmem_limit_bytes=16 * 2**20),
    )


def lanes(start, size=128):
    return pl.ds(pl.multiple_of(start, 128), size)


def rows(start, size):
    return pl.ds(pl.multiple_of(start, 16), size)


def place_columns(out, j, part):
    out[:, j * 64 : j * 64 + 64] = part[:, :64]
    out[:, 256 + j * 64 : 256 + j * 64 + 64] = part[:, 64:]


def cut_coupling_body(ref, *outs):
    z = lax.axis_index("z")
    for k, out in enumerate(outs):
        for j in range(4):
            place_columns(out, j, ref[:, lanes((z ^ k) * 512 + j * 128)])


def cut_inverse_body(ref, mine, theirs, *outs):
    y, c = lax.axis_index("y"), lax.axis_index("c")
    for k, out in enumerate(outs):
        for j in range(4):
            place_columns(out, j, ref[:, lanes(j * 512 + (y ^ k) * 128)])
        out[:, 512:576] = jnp.where(c == 0, mine[...], theirs[...])
        out[:, 576:640] = jnp.where(c == 0, theirs[...], mine[...])


def stack_body(*refs):
    z, y = lax.axis_index("z"), lax.axis_index("y")
    block, entering, scratch = refs[8:]
    for k in range(4):
        block[0, rows((z ^ k) * 64, 64), :] = refs[k][...]
        block[1, rows((y ^ k) * 64, 64), :] = refs[4 + k][:, :512]
        scratch[y ^ k] = refs[4 + k][:, 512:]
    for j in range(4):
        place_columns(entering, j, scratch[j])


def split(value):
    high = value.astype(bf16)
    return high, (value - high.astype(f32)).astype(bf16)


def product(value, operator):
    def dot(a, b):
        return lax.dot_general(a, b, contract_last, preferred_element_type=f32)

    vh, vl = split(value)
    oh, ol = split(operator)
    return dot(vh, oh) + (dot(vh, ol) + dot(vl, oh))


def natural_columns(ref, y):
    parts = []
    for core in range(2):
        wide = ref[:, lanes(core * 256 + lax.shift_right_logical(y, 1) * 128)]
        parts.append(jnp.where((y & 1) == 0, wide[:, :64], wide[:, 64:]))
    return jnp.concatenate(parts, axis=1)


def add_up(refs):
    total = refs[0][...]
    for ref in refs[1:]:
        total = total + ref[...]
    return total


def couple_body(n_parts, *refs):
    parts, (load, w0, w1), outs = refs[:n_parts], refs[n_parts : n_parts + 3], refs[n_parts + 3 :]
    out = outs[0]
    entering = add_up(parts)
    if n_parts > 1:
        total = outs[2]
        total[...] = entering
        outs[1][...] = natural_columns(total, lax.axis_index("y"))
    out[:, :256] = -product(entering, w0[...])
    out[:, 256:] = -product(entering, w1[...])
    own = rows(lax.axis_index("z") * 16, 16)
    out[own, :] = out[own, :] + load[...]


def invert_body(last, a0, a1, a2, a3, w0, w1, out, *pieces):
    corrected = add_up((a0, a1, a2, a3))
    out[:, :256] = product(corrected, w0[...])
    out[:, 256:] = product(corrected, w1[...])
    if last:
        y = lax.axis_index("y")
        for k, piece in enumerate(pieces):
            piece[...] = natural_columns(out, y ^ k)


def lift_body(current, lift, *refs):
    outs, lifted = refs[:4], refs[4]
    x = lax.axis_index("x")
    for j in range(4):
        lifted[:, j * 512 : (j + 1) * 512] = product(current[...], lift[j * 512 : (j + 1) * 512, :])
    for k, out in enumerate(outs):
        to = lax.rem(x + k, 4)
        for j in range(4):
            place_columns(out, j, lifted[:, lanes(j * 512 + to * 128)])


def finish_body(a0, a1, a2, a3, theirs, out):
    x, c = lax.axis_index("x"), lax.axis_index("c")
    for k, part in enumerate((a0, a1, a2, a3)):
        for z0 in range(4):
            mine = part[z0 * 16 : z0 * 16 + 16, :]
            other = theirs[k, z0 * 16 : z0 * 16 + 16, :]
            base = z0 * 128 + (x ^ k) * 32
            out[0, rows(base + c * 16, 16), :] = jnp.where(c == 0, mine[:, :64], mine[:, 64:])
            out[0, rows(base + (1 - c) * 16, 16), :] = jnp.where(c == 0, other[:, :64], other[:, 64:])


def after(values, done):
    return lax.optimization_barrier((values, done))[0]


def on_device(sources, leaf_ops, edge_slot, merge_ops, lift_ops, coupling, inverse, boundary):
    x, z, y, c = (lax.axis_index(axis) for axis in ("x", "z", "y", "c"))
    slot = edge_slot[0, 0]
    merge = merge_ops[0, 0]
    leaf = leaf_ops[0, 0]

    def part_of(value, bit, size):
        given = lax.dynamic_slice_in_dim(value, (1 - bit) * size, size, 0)
        return given, lax.dynamic_slice_in_dim(value, bit * size, size, 0)

    with jax.named_scope("boundary"):
        by_box = boundary.reshape(4, 4, 2, 16, 64)
        of_plane = lax.dynamic_index_in_dim(by_box, x, 1, keepdims=False)
        mine = lax.dynamic_index_in_dim(of_plane, c, 1, keepdims=False).reshape(64, 64)
        other = lax.dynamic_index_in_dim(of_plane, 1 - c, 1, keepdims=False).reshape(64, 64)
        theirs = swap(other, "c", 1)

    with jax.named_scope("reduction"):
        onehot = (slot[:, None] == jnp.arange(256, dtype=jnp.int32)[None, :]).astype(f32)
        merge_first = lax.dot_general(
            merge, onehot, (((1,), (0,)), ((), ())), precision=lax.Precision.HIGHEST, preferred_element_type=f32
        )
        given, kept = part_of(sources[0, 0], z >> 1, 256)
        given_on, given_kept = part_of(dot_t(given, leaf, None), z & 1, 128)
        given_on = dot_t(given_on, merge_first)
        given_kept = dot_t(given_kept, merge_first)

    with jax.named_scope("operators"):
        c_pieces = local_kernel(cut_coupling_body, [(64, 512)] * 4)(coupling[0])
        i_pieces = local_kernel(cut_inverse_body, [(64, 640)] * 4)(inverse[0], mine, theirs)
        arrived = (
            [c_pieces[0]]
            + [swap(c_pieces[k], "z", k) for k in (1, 2, 3)]
            + [i_pieces[0]]
            + [swap(i_pieces[k], "y", k) for k in (1, 2, 3)]
        )
        arrived = after(arrived, given_kept)
        block, entering = local_kernel(stack_body, [(2, 256, 512), (64, 512)], scratch=[(4, 64, 128)])(*arrived)
        operators = lax.all_gather(block, ("x", "c"), axis=0)

    with jax.named_scope("reduction"):
        sent_on = swap(given_on, "z", 2)
        sent_kept = swap(given_kept, "z", 2)
        kept_on, kept_kept = part_of(dot_t(kept, leaf, None), z & 1, 128)
        kept_on = dot_t(kept_on, merge_first) + sent_on
        kept_kept = dot_t(kept_kept, merge_first) + sent_kept
        current = dot_t(kept_kept, merge) + swap(dot_t(kept_on, merge), "z", 1)
        for axis, mask, bit in (("y", 2, y >> 1), ("y", 1, y & 1), ("c", 1, c)):
            given, kept = part_of(current, bit, current.shape[0] // 2)
            current = dot_t(kept, merge) + swap(dot_t(given, merge), axis, mask)

    with jax.named_scope("loads"):
        l_pieces = local_kernel(lift_body, [(16, 512)] * 4, 3 * 2 * 16 * 256 * 2048, 2**21, [(16, 2048)])(
            current, lift_ops[0, 0]
        )
        arrived = []
        for k in range(4):
            pairs = [(s * 4 + y0, y0 * 4 + (s + k) % 4) for s in range(4) for y0 in range(4)]
            arrived.append(lax.ppermute(l_pieces[k], ("x", "y"), pairs))
        loads = [select(arrived, (y - s) % 4) for s in range(4)]

    with jax.named_scope("chain"):
        solutions = []
        flops = 3 * 2 * 64 * 512 * 512
        parts = [entering]
        for s in range(4):
            out_shapes = [(64, 512)] + ([(64, 128)] if s else [])
            couple = local_kernel(
                functools.partial(couple_body, len(parts)), out_shapes, flops, 2**21, [(64, 512)] if s else []
            )
            of_slab = after(operators, partial) if s else operators
            results = couple(*parts, loads[s], of_slab[2 * s, 0], of_slab[2 * s + 1, 0])
            solutions += results[1:]
            partial = results[0]
            parts = [partial] + [swap(partial, "z", k) for k in (1, 2, 3)]
            invert = local_kernel(
                functools.partial(invert_body, s == 3),
                [(64, 512)] + ([(64, 128)] * 4 if s == 3 else []),
                flops,
                2**21,
            )
            of_slab = after(operators, partial)
            results = invert(*parts, of_slab[2 * s, 1], of_slab[2 * s + 1, 1])
            partial = results[0]
            if s < 3:
                parts = [partial] + [swap(partial, "y", k) for k in (1, 2, 3)]
            else:
                parts = [results[1]] + [swap(results[1 + k], "y", k) for k in (1, 2, 3)]
                solutions.append((parts[0] + parts[1]) + (parts[2] + parts[3]))

    with jax.named_scope("output"):
        parts = [select(solutions, x)] + [swap(select(solutions, x ^ k), "x", k) for k in (1, 2, 3)]
        theirs = swap(jnp.stack(parts), "c", 1)
        return local_kernel(finish_body, [(1, 512, 64)])(*parts, theirs)[0]


def solution(mesh):
    wide = Mesh(mesh.devices.reshape(4, 4, 4, 2), ("x", "z", "y", "c"))
    box = ("z", "y", "c")
    return jax.shard_map(
        on_device,
        mesh=wide,
        in_specs=(
            P("x", box, None, None),
            P("x", box, None, None),
            P("x", box, None),
            P("x", box, None, None),
            P("x", box, None, None),
            P("x", box, None),
            P("x", box, None),
            P(None, box),
        ),
        out_specs=P("x", None, box),
        check_vma=False,
    )
```

```python
import functools

import jax
import jax.numpy as jnp
from jax import lax
from jax.experimental import pallas as pl
from jax.experimental.pallas import tpu as pltpu
from jax.sharding import Mesh, PartitionSpec as P

contract_last = (((1,), (1,)), ((), ()))
f32 = jnp.float32
bf16 = jnp.bfloat16
sent = (0, 2, 3, 1)


def dot_t(a, b, precision=lax.Precision.HIGH):
    return lax.dot_general(a, b, contract_last, precision=precision, preferred_element_type=f32)


def swap(value, axis, mask):
    count = 2 if axis == "c" else 4
    return lax.ppermute(value, axis, [(i, i ^ mask) for i in range(count)])


def exchange(pieces, axis):
    return [pieces[0]] + [swap(pieces[k], axis, k) for k in sent[1:]]


def select(choices, index):
    chosen = choices[0]
    for k in range(1, len(choices)):
        chosen = jnp.where(index == k, choices[k], chosen)
    return chosen


def local_kernel(body, out_shapes, flops=0, bytes_accessed=2**20, scratch=()):
    return pl.pallas_call(
        body,
        out_shape=[jax.ShapeDtypeStruct(shape, f32) for shape in out_shapes],
        scratch_shapes=[pltpu.VMEM(shape, f32) for shape in scratch],
        cost_estimate=pl.CostEstimate(flops=flops, bytes_accessed=bytes_accessed, transcendentals=0),
        compiler_params=pltpu.CompilerParams(vmem_limit_bytes=16 * 2**20),
    )


def lanes(start, size=128):
    return pl.ds(pl.multiple_of(start, 128), size)


def rows(start, size):
    return pl.ds(pl.multiple_of(start, 16), size)


def place_columns(out, j, part):
    out[:, j * 64 : j * 64 + 64] = part[:, :64]
    out[:, 256 + j * 64 : 256 + j * 64 + 64] = part[:, 64:]


def cut_body(c_ref, i_ref, *outs):
    z, y = lax.axis_index("z"), lax.axis_index("y")
    for k in range(4):
        for j in range(4):
            place_columns(outs[k], j, c_ref[:, lanes((z ^ k) * 512 + j * 128)])
            place_columns(outs[4 + k], j, i_ref[:, lanes(j * 512 + (y ^ k) * 128)])


def stack_body(*refs):
    z, y = lax.axis_index("z"), lax.axis_index("y")
    block = refs[8]
    for i, k in enumerate(sent):
        block[0, rows((z ^ k) * 64, 64), :] = refs[i][...]
        block[1, rows((y ^ k) * 64, 64), :] = refs[4 + i][...]


def widen_body(a0, a1, a2, a3, out, scratch):
    y = lax.axis_index("y")
    for k, part in zip(sent, (a0, a1, a2, a3)):
        scratch[y ^ k] = part[...]
    for j in range(4):
        place_columns(out, j, scratch[j])


def split(value):
    high = value.astype(bf16)
    return high, (value - high.astype(f32)).astype(bf16)


def product(value, operator):
    def dot(a, b):
        return lax.dot_general(a, b, contract_last, preferred_element_type=f32)

    vh, vl = split(value)
    oh, ol = split(operator)
    return dot(vh, oh) + (dot(vh, ol) + dot(vl, oh))


def natural_columns(ref, y):
    parts = []
    for core in range(2):
        wide = ref[:, lanes(core * 256 + lax.shift_right_logical(y, 1) * 128)]
        parts.append(jnp.where((y & 1) == 0, wide[:, :64], wide[:, 64:]))
    return jnp.concatenate(parts, axis=1)


def add_up(refs):
    total = refs[0][...]
    for ref in refs[1:]:
        total = total + ref[...]
    return total


def couple_body(n_parts, *refs):
    parts, (load, w0, w1), outs = refs[:n_parts], refs[n_parts : n_parts + 3], refs[n_parts + 3 :]
    out = outs[0]
    entering = add_up(parts)
    if n_parts > 1:
        total = outs[2]
        total[...] = entering
        outs[1][...] = natural_columns(total, lax.axis_index("y"))
    out[:, :256] = -product(entering, w0[...])
    out[:, 256:] = -product(entering, w1[...])
    own = rows(lax.axis_index("z") * 16, 16)
    out[own, :] = out[own, :] + load[...]


def invert_body(last, a0, a1, a2, a3, w0, w1, out, *pieces):
    corrected = add_up((a0, a1, a2, a3))
    out[:, :256] = product(corrected, w0[...])
    out[:, 256:] = product(corrected, w1[...])
    if last:
        y = lax.axis_index("y")
        for k, piece in enumerate(pieces):
            piece[...] = natural_columns(out, y ^ k)


def lift_body(current, lift, *refs):
    outs, lifted = refs[:4], refs[4]
    x = lax.axis_index("x")
    for j in range(4):
        lifted[:, j * 512 : (j + 1) * 512] = product(current[...], lift[j * 512 : (j + 1) * 512, :])
    for k, out in enumerate(outs):
        to = lax.rem(x + k, 4)
        for j in range(4):
            place_columns(out, j, lifted[:, lanes(j * 512 + to * 128)])


def finish_body(a0, a1, a2, a3, theirs, out):
    x, c = lax.axis_index("x"), lax.axis_index("c")
    for i, part in enumerate((a0, a1, a2, a3)):
        k = sent[i]
        for z0 in range(4):
            mine = part[z0 * 16 : z0 * 16 + 16, :]
            other = theirs[i, z0 * 16 : z0 * 16 + 16, :]
            base = z0 * 128 + (x ^ k) * 32
            out[0, rows(base + c * 16, 16), :] = jnp.where(c == 0, mine[:, :64], mine[:, 64:])
            out[0, rows(base + (1 - c) * 16, 16), :] = jnp.where(c == 0, other[:, :64], other[:, 64:])


def after(values, done):
    return lax.optimization_barrier((values, done))[0]


def on_device(sources, leaf_ops, edge_slot, merge_ops, lift_ops, coupling, inverse, boundary):
    x, z, y, c = (lax.axis_index(axis) for axis in ("x", "z", "y", "c"))
    slot = edge_slot[0, 0]
    merge = merge_ops[0, 0]
    leaf = leaf_ops[0, 0]

    def part_of(value, bit, size):
        given = lax.dynamic_slice_in_dim(value, (1 - bit) * size, size, 0)
        return given, lax.dynamic_slice_in_dim(value, bit * size, size, 0)

    with jax.named_scope("reduction"):
        onehot = (slot[:, None] == jnp.arange(256, dtype=jnp.int32)[None, :]).astype(f32)
        merge_first = lax.dot_general(
            merge, onehot, (((1,), (0,)), ((), ())), precision=lax.Precision.HIGHEST, preferred_element_type=f32
        )
        given, kept = part_of(sources[0, 0], z >> 1, 256)
        given_on, given_kept = part_of(dot_t(given, leaf, None), z & 1, 128)
        given_on = dot_t(given_on, merge_first)
        given_kept = dot_t(given_kept, merge_first)

    with jax.named_scope("operators"):
        pieces = local_kernel(cut_body, [(64, 512)] * 8)(coupling[0], inverse[0])
        arrived = exchange(pieces[:4], "z") + exchange(pieces[4:], "y")
        block = local_kernel(stack_body, [(2, 256, 512)])(*after(arrived, given_kept))[0]
        operators = lax.all_gather(block, ("x", "c"), axis=0)

    with jax.named_scope("reduction"):
        sent_on = swap(given_on, "z", 2)
        sent_kept = swap(given_kept, "z", 2)
        kept_on, kept_kept = part_of(dot_t(kept, leaf, None), z & 1, 128)
        kept_on = dot_t(kept_on, merge_first) + sent_on
        kept_kept = dot_t(kept_kept, merge_first) + sent_kept
        current = dot_t(kept_kept, merge) + swap(dot_t(kept_on, merge), "z", 1)
        given, kept = part_of(current, y >> 1, 64)
        level2 = dot_t(kept, merge) + swap(dot_t(given, merge), "y", 2)

    with jax.named_scope("boundary"):
        by_box = boundary.reshape(4, 4, 2, 16, 64)
        of_plane = lax.dynamic_index_in_dim(by_box, x, 1, keepdims=False)
        mine = lax.dynamic_index_in_dim(of_plane, c, 1, keepdims=False).reshape(64, 64)
        other = lax.dynamic_index_in_dim(of_plane, 1 - c, 1, keepdims=False).reshape(64, 64)
        theirs = swap(after(other, current), "c", 1)
        wide = jnp.concatenate([jnp.where(c == 0, mine, theirs), jnp.where(c == 0, theirs, mine)], axis=1)
        entering_parts = exchange([after(wide, level2)] * 4, "y")

    with jax.named_scope("reduction"):
        given, kept = part_of(level2, y & 1, 32)
        level3 = dot_t(kept, merge) + swap(dot_t(given, merge), "y", 1)
        given, kept = part_of(level3, c, 16)
        current = dot_t(kept, merge) + swap(dot_t(given, merge), "c", 1)

    with jax.named_scope("boundary"):
        entering = local_kernel(widen_body, [(64, 512)], scratch=[(4, 64, 128)])(*entering_parts)[0]

    with jax.named_scope("loads"):
        l_pieces = local_kernel(lift_body, [(16, 512)] * 4, 3 * 2 * 16 * 256 * 2048, 2**21, [(16, 2048)])(
            current, lift_ops[0, 0]
        )
        arrived = []
        for k in range(4):
            pairs = [(s * 4 + y0, y0 * 4 + (s + k) % 4) for s in range(4) for y0 in range(4)]
            arrived.append(lax.ppermute(l_pieces[k], ("x", "y"), pairs))
        loads = [select(arrived, (y - s) % 4) for s in range(4)]

    with jax.named_scope("chain"):
        solutions = []
        flops = 3 * 2 * 64 * 512 * 512
        parts = [entering]
        for s in range(4):
            out_shapes = [(64, 512)] + ([(64, 128)] if s else [])
            couple = local_kernel(
                functools.partial(couple_body, len(parts)), out_shapes, flops, 2**21, [(64, 512)] if s else []
            )
            of_slab = after(operators, partial) if s else operators
            results = couple(*parts, loads[s], of_slab[2 * s, 0], of_slab[2 * s + 1, 0])
            solutions += results[1:]
            partial = results[0]
            parts = exchange([partial] * 4, "z")
            invert = local_kernel(
                functools.partial(invert_body, s == 3),
                [(64, 512)] + ([(64, 128)] * 4 if s == 3 else []),
                flops,
                2**21,
            )
            of_slab = after(operators, partial)
            results = invert(*parts, of_slab[2 * s, 1], of_slab[2 * s + 1, 1])
            partial = results[0]
            if s < 3:
                parts = exchange([partial] * 4, "y")
            else:
                parts = exchange(results[1:], "y")
                solutions.append((parts[0] + parts[1]) + (parts[2] + parts[3]))

    with jax.named_scope("output"):
        parts = exchange([select(solutions, x ^ k) for k in range(4)], "x")
        theirs = swap(jnp.stack(parts), "c", 1)
        return local_kernel(finish_body, [(1, 512, 64)])(*parts, theirs)[0]


def solution(mesh):
    wide = Mesh(mesh.devices.reshape(4, 4, 4, 2), ("x", "z", "y", "c"))
    box = ("z", "y", "c")
    return jax.shard_map(
        on_device,
        mesh=wide,
        in_specs=(
            P("x", box, None, None),
            P("x", box, None, None),
            P("x", box, None),
            P("x", box, None, None),
            P("x", box, None, None),
            P("x", box, None),
            P("x", box, None),
            P(None, box),
        ),
        out_specs=P("x", None, box),
        check_vma=False,
    )
```

```python
import functools

import jax
import jax.numpy as jnp
from jax import lax
from jax.experimental import pallas as pl
from jax.experimental.pallas import tpu as pltpu
from jax.sharding import Mesh, PartitionSpec as P

contract_last = (((1,), (1,)), ((), ()))
f32 = jnp.float32
bf16 = jnp.bfloat16
sent = (0, 3, 2, 1)


def dot_t(a, b, precision=lax.Precision.HIGH):
    return lax.dot_general(a, b, contract_last, precision=precision, preferred_element_type=f32)


def swap(value, axis, mask):
    count = 2 if axis == "c" else 4
    return lax.ppermute(value, axis, [(i, i ^ mask) for i in range(count)])


def exchange(pieces, axis):
    return [pieces[0]] + [swap(pieces[k], axis, k) for k in sent[1:]]


def select(choices, index):
    chosen = choices[0]
    for k in range(1, len(choices)):
        chosen = jnp.where(index == k, choices[k], chosen)
    return chosen


def local_kernel(body, out_shapes, flops=0, bytes_accessed=2**20, scratch=()):
    return pl.pallas_call(
        body,
        out_shape=[jax.ShapeDtypeStruct(shape, f32) for shape in out_shapes],
        scratch_shapes=[pltpu.VMEM(shape, f32) for shape in scratch],
        cost_estimate=pl.CostEstimate(flops=flops, bytes_accessed=bytes_accessed, transcendentals=0),
        compiler_params=pltpu.CompilerParams(vmem_limit_bytes=16 * 2**20),
    )


def lanes(start, size=128):
    return pl.ds(pl.multiple_of(start, 128), size)


def rows(start, size):
    return pl.ds(pl.multiple_of(start, 16), size)


def place_columns(out, j, part):
    out[:, j * 64 : j * 64 + 64] = part[:, :64]
    out[:, 256 + j * 64 : 256 + j * 64 + 64] = part[:, 64:]


def cut_body(c_ref, i_ref, *outs):
    z, y = lax.axis_index("z"), lax.axis_index("y")
    for k in range(4):
        for j in range(4):
            place_columns(outs[k], j, c_ref[:, lanes((z ^ k) * 512 + j * 128)])
            place_columns(outs[4 + k], j, i_ref[:, lanes(j * 512 + (y ^ k) * 128)])


def stack_body(*refs):
    z, y = lax.axis_index("z"), lax.axis_index("y")
    block = refs[8]
    for i, k in enumerate(sent):
        block[0, rows((z ^ k) * 64, 64), :] = refs[2 * i][...]
        block[1, rows((y ^ k) * 64, 64), :] = refs[2 * i + 1][...]


def widen_body(a0, a1, a2, a3, out, scratch):
    y = lax.axis_index("y")
    for k, part in zip(sent, (a0, a1, a2, a3)):
        scratch[y ^ k] = part[...]
    for j in range(4):
        place_columns(out, j, scratch[j])


def split(value):
    high = value.astype(bf16)
    return high, (value - high.astype(f32)).astype(bf16)


def product(value, operator):
    def dot(a, b):
        return lax.dot_general(a, b, contract_last, preferred_element_type=f32)

    vh, vl = split(value)
    oh, ol = split(operator)
    return dot(vh, oh) + (dot(vh, ol) + dot(vl, oh))


def natural_columns(ref, y):
    parts = []
    for core in range(2):
        wide = ref[:, lanes(core * 256 + lax.shift_right_logical(y, 1) * 128)]
        parts.append(jnp.where((y & 1) == 0, wide[:, :64], wide[:, 64:]))
    return jnp.concatenate(parts, axis=1)


def add_up(refs):
    total = refs[0][...]
    for ref in refs[1:]:
        total = total + ref[...]
    return total


def couple_body(n_parts, *refs):
    parts, (load, w0, w1), outs = refs[:n_parts], refs[n_parts : n_parts + 3], refs[n_parts + 3 :]
    out = outs[0]
    entering = add_up(parts)
    if n_parts > 1:
        total = outs[2]
        total[...] = entering
        outs[1][...] = natural_columns(total, lax.axis_index("y"))
    out[:, :256] = -product(entering, w0[...])
    out[:, 256:] = -product(entering, w1[...])
    own = rows(lax.axis_index("z") * 16, 16)
    out[own, :] = out[own, :] + load[...]


def invert_body(last, a0, a1, a2, a3, w0, w1, out, *pieces):
    corrected = add_up((a0, a1, a2, a3))
    out[:, :256] = product(corrected, w0[...])
    out[:, 256:] = product(corrected, w1[...])
    if last:
        y = lax.axis_index("y")
        for k, piece in enumerate(pieces):
            piece[...] = natural_columns(out, y ^ k)


def lift_body(current, lift, *refs):
    outs, lifted = refs[:4], refs[4]
    x = lax.axis_index("x")
    for j in range(4):
        lifted[:, j * 512 : (j + 1) * 512] = product(current[...], lift[j * 512 : (j + 1) * 512, :])
    for k, out in enumerate(outs):
        to = lax.rem(x + k, 4)
        for j in range(4):
            place_columns(out, j, lifted[:, lanes(j * 512 + to * 128)])


def finish_body(a0, a1, a2, a3, theirs, turned, out):
    x, c = lax.axis_index("x"), lax.axis_index("c")
    for i, part in enumerate((a0, a1, a2, a3)):
        k = sent[i]
        for z0 in range(4):
            mine = part[z0 * 16 : z0 * 16 + 16, :]
            other = theirs[i, z0 * 16 : z0 * 16 + 16, :]
            base = z0 * 128 + (x ^ k) * 32
            out[rows(base + c * 16, 16), :] = jnp.where(c == 0, mine[:, :64], mine[:, 64:])
            out[rows(base + (1 - c) * 16, 16), :] = jnp.where(c == 0, other[:, :64], other[:, 64:])
    turned[0, :, :] = out[...].T


def after(values, done):
    return lax.optimization_barrier((values, done))[0]


def on_device(sources, leaf_ops, edge_slot, merge_ops, lift_ops, coupling, inverse, boundary):
    x, z, y, c = (lax.axis_index(axis) for axis in ("x", "z", "y", "c"))
    slot = edge_slot[0, 0]
    merge = merge_ops[0, 0]
    leaf = leaf_ops[0, 0]

    def part_of(value, bit, size):
        given = lax.dynamic_slice_in_dim(value, (1 - bit) * size, size, 0)
        return given, lax.dynamic_slice_in_dim(value, bit * size, size, 0)

    with jax.named_scope("reduction"):
        onehot = (slot[:, None] == jnp.arange(256, dtype=jnp.int32)[None, :]).astype(f32)
        merge_first = lax.dot_general(
            merge, onehot, (((1,), (0,)), ((), ())), precision=lax.Precision.HIGHEST, preferred_element_type=f32
        )
        given, kept = part_of(sources[0, 0], z >> 1, 256)
        given_on, given_kept = part_of(dot_t(given, leaf, None), z & 1, 128)
        given_on = dot_t(given_on, merge_first)
        given_kept = dot_t(given_kept, merge_first)

    with jax.named_scope("operators"):
        pieces = local_kernel(cut_body, [(64, 512)] * 8)(coupling[0], inverse[0])
        arrived = []
        for k in sent:
            arrived += [swap(pieces[k], "z", k) if k else pieces[0], swap(pieces[4 + k], "y", k) if k else pieces[4]]
        block = local_kernel(stack_body, [(2, 256, 512)])(*after(arrived, given_kept))[0]
        operators = lax.all_gather(block, ("x", "c"), axis=0)

    with jax.named_scope("reduction"):
        sent_on = swap(given_on, "z", 2)
        sent_kept = swap(given_kept, "z", 2)
        kept_on, kept_kept = part_of(dot_t(kept, leaf, None), z & 1, 128)
        kept_on = dot_t(kept_on, merge_first) + sent_on
        kept_kept = dot_t(kept_kept, merge_first) + sent_kept
        current = dot_t(kept_kept, merge) + swap(dot_t(kept_on, merge), "z", 1)
        given, kept = part_of(current, y >> 1, 64)
        level2 = dot_t(kept, merge) + swap(dot_t(given, merge), "y", 2)

    with jax.named_scope("boundary"):
        by_box = boundary.reshape(4, 4, 2, 16, 64)
        of_plane = lax.dynamic_index_in_dim(by_box, x, 1, keepdims=False)
        mine = lax.dynamic_index_in_dim(of_plane, c, 1, keepdims=False).reshape(64, 64)
        other = lax.dynamic_index_in_dim(of_plane, 1 - c, 1, keepdims=False).reshape(64, 64)
        theirs = swap(after(other, current), "c", 1)
        wide = jnp.concatenate([jnp.where(c == 0, mine, theirs), jnp.where(c == 0, theirs, mine)], axis=1)
        entering_parts = exchange([after(wide, level2)] * 4, "y")

    with jax.named_scope("reduction"):
        given, kept = part_of(level2, y & 1, 32)
        level3 = dot_t(kept, merge) + swap(dot_t(given, merge), "y", 1)
        given, kept = part_of(level3, c, 16)
        current = dot_t(kept, merge) + swap(dot_t(given, merge), "c", 1)

    with jax.named_scope("boundary"):
        entering = local_kernel(widen_body, [(64, 512)], scratch=[(4, 64, 128)])(*entering_parts)[0]

    with jax.named_scope("loads"):
        l_pieces = local_kernel(lift_body, [(16, 512)] * 4, 3 * 2 * 16 * 256 * 2048, 2**21, [(16, 2048)])(
            current, lift_ops[0, 0]
        )
        arrived = []
        for k in range(4):
            pairs = [(s * 4 + y0, y0 * 4 + (s + k) % 4) for s in range(4) for y0 in range(4)]
            arrived.append(lax.ppermute(l_pieces[k], ("x", "y"), pairs))
        loads = [select(arrived, (y - s) % 4) for s in range(4)]

    with jax.named_scope("chain"):
        solutions = []
        flops = 3 * 2 * 64 * 512 * 512
        parts = [entering]
        for s in range(4):
            out_shapes = [(64, 512)] + ([(64, 128)] if s else [])
            couple = local_kernel(
                functools.partial(couple_body, len(parts)), out_shapes, flops, 2**21, [(64, 512)] if s else []
            )
            of_slab = after(operators, partial) if s else operators
            results = couple(*parts, loads[s], of_slab[2 * s, 0], of_slab[2 * s + 1, 0])
            solutions += results[1:]
            partial = results[0]
            parts = exchange([partial] * 4, "z")
            invert = local_kernel(
                functools.partial(invert_body, s == 3),
                [(64, 512)] + ([(64, 128)] * 4 if s == 3 else []),
                flops,
                2**21,
            )
            of_slab = after(operators, partial)
            results = invert(*parts, of_slab[2 * s, 1], of_slab[2 * s + 1, 1])
            partial = results[0]
            if s < 3:
                parts = exchange([partial] * 4, "y")
            else:
                parts = exchange(results[1:], "y")
                solutions.append((parts[0] + parts[1]) + (parts[2] + parts[3]))

    with jax.named_scope("output"):
        parts = exchange([select(solutions, x ^ k) for k in range(4)], "x")
        theirs = swap(jnp.stack(parts), "c", 1)
        turned = local_kernel(finish_body, [(1, 64, 512)], scratch=[(512, 64)])(*parts, theirs)[0]
        return turned.transpose(0, 2, 1)


def solution(mesh):
    wide = Mesh(mesh.devices.reshape(4, 4, 4, 2), ("x", "z", "y", "c"))
    box = ("z", "y", "c")
    return jax.shard_map(
        on_device,
        mesh=wide,
        in_specs=(
            P("x", box, None, None),
            P("x", box, None, None),
            P("x", box, None),
            P("x", box, None, None),
            P("x", box, None, None),
            P("x", box, None),
            P("x", box, None),
            P(None, box),
        ),
        out_specs=P("x", None, box),
        check_vma=False,
    )
```

```python
import functools

import jax
import jax.numpy as jnp
from jax import lax
from jax.experimental import pallas as pl
from jax.experimental.pallas import tpu as pltpu
from jax.sharding import Mesh, PartitionSpec as P

contract_last = (((1,), (1,)), ((), ()))
f32 = jnp.float32
bf16 = jnp.bfloat16
sent = (0, 3, 2, 1)


def dot_t(a, b, precision=lax.Precision.HIGH):
    return lax.dot_general(a, b, contract_last, precision=precision, preferred_element_type=f32)


def swap(value, axis, mask):
    count = 2 if axis == "c" else 4
    return lax.ppermute(value, axis, [(i, i ^ mask) for i in range(count)])


def exchange(pieces, axis):
    return [pieces[0]] + [swap(pieces[k], axis, k) for k in sent[1:]]


def select(choices, index):
    chosen = choices[0]
    for k in range(1, len(choices)):
        chosen = jnp.where(index == k, choices[k], chosen)
    return chosen


def local_kernel(body, out_shapes, flops=0, bytes_accessed=2**20, scratch=()):
    return pl.pallas_call(
        body,
        out_shape=[jax.ShapeDtypeStruct(shape, f32) for shape in out_shapes],
        scratch_shapes=[pltpu.VMEM(shape, f32) for shape in scratch],
        cost_estimate=pl.CostEstimate(flops=flops, bytes_accessed=bytes_accessed, transcendentals=0),
        compiler_params=pltpu.CompilerParams(vmem_limit_bytes=16 * 2**20),
    )


def lanes(start, size=128):
    return pl.ds(pl.multiple_of(start, 128), size)


def rows(start, size):
    return pl.ds(pl.multiple_of(start, 16), size)


def place_columns(out, j, part):
    out[:, j * 64 : j * 64 + 64] = part[:, :64]
    out[:, 256 + j * 64 : 256 + j * 64 + 64] = part[:, 64:]


def cut_body(c_hbm, i_hbm, *refs):
    outs, c_ref, i_ref, sems = refs[:8], refs[8], refs[9], refs[10]
    c_copy = pltpu.make_async_copy(c_hbm, c_ref, sems.at[0])
    i_copy = pltpu.make_async_copy(i_hbm, i_ref, sems.at[1])
    c_copy.start()
    i_copy.start()
    z, y = lax.axis_index("z"), lax.axis_index("y")
    c_copy.wait()
    for k in range(4):
        for j in range(4):
            place_columns(outs[k], j, c_ref[:, lanes((z ^ k) * 512 + j * 128)])
    i_copy.wait()
    for k in range(4):
        for j in range(4):
            place_columns(outs[4 + k], j, i_ref[:, lanes(j * 512 + (y ^ k) * 128)])


def stack_body(*refs):
    z, y = lax.axis_index("z"), lax.axis_index("y")
    block = refs[8]
    for i, k in enumerate(sent):
        block[0, rows((z ^ k) * 64, 64), :] = refs[2 * i][...]
        block[1, rows((y ^ k) * 64, 64), :] = refs[2 * i + 1][...]


def widen_body(a0, a1, a2, a3, out, scratch):
    y = lax.axis_index("y")
    for k, part in zip(sent, (a0, a1, a2, a3)):
        scratch[y ^ k] = part[...]
    for j in range(4):
        place_columns(out, j, scratch[j])


def split(value):
    high = value.astype(bf16)
    return high, (value - high.astype(f32)).astype(bf16)


def product(value, operator):
    def dot(a, b):
        return lax.dot_general(a, b, contract_last, preferred_element_type=f32)

    vh, vl = split(value)
    oh, ol = split(operator)
    return dot(vh, oh) + (dot(vh, ol) + dot(vl, oh))


def natural_columns(ref, y):
    parts = []
    for core in range(2):
        wide = ref[:, lanes(core * 256 + lax.shift_right_logical(y, 1) * 128)]
        parts.append(jnp.where((y & 1) == 0, wide[:, :64], wide[:, 64:]))
    return jnp.concatenate(parts, axis=1)


def add_up(refs):
    total = refs[0][...]
    for ref in refs[1:]:
        total = total + ref[...]
    return total


def couple_body(n_parts, *refs):
    parts, (load, w0, w1), outs = refs[:n_parts], refs[n_parts : n_parts + 3], refs[n_parts + 3 :]
    out = outs[0]
    entering = add_up(parts)
    if n_parts > 1:
        total = outs[2]
        total[...] = entering
        outs[1][...] = natural_columns(total, lax.axis_index("y"))
    out[:, :256] = -product(entering, w0[...])
    out[:, 256:] = -product(entering, w1[...])
    own = rows(lax.axis_index("z") * 16, 16)
    out[own, :] = out[own, :] + load[...]


def invert_body(last, a0, a1, a2, a3, w0, w1, out, *pieces):
    corrected = add_up((a0, a1, a2, a3))
    out[:, :256] = product(corrected, w0[...])
    out[:, 256:] = product(corrected, w1[...])
    if last:
        y = lax.axis_index("y")
        for k, piece in enumerate(pieces):
            piece[...] = natural_columns(out, y ^ k)


def lift_body(current, lift, *refs):
    outs, lifted = refs[:4], refs[4]
    x = lax.axis_index("x")
    for j in range(4):
        lifted[:, j * 512 : (j + 1) * 512] = product(current[...], lift[j * 512 : (j + 1) * 512, :])
    for k, out in enumerate(outs):
        to = lax.rem(x + k, 4)
        for j in range(4):
            place_columns(out, j, lifted[:, lanes(j * 512 + to * 128)])


def finish_body(a0, a1, a2, a3, theirs, turned, out):
    x, c = lax.axis_index("x"), lax.axis_index("c")
    for i, part in enumerate((a0, a1, a2, a3)):
        k = sent[i]
        for z0 in range(4):
            mine = part[z0 * 16 : z0 * 16 + 16, :]
            other = theirs[i, z0 * 16 : z0 * 16 + 16, :]
            base = z0 * 128 + (x ^ k) * 32
            out[rows(base + c * 16, 16), :] = jnp.where(c == 0, mine[:, :64], mine[:, 64:])
            out[rows(base + (1 - c) * 16, 16), :] = jnp.where(c == 0, other[:, :64], other[:, 64:])
    turned[0, :, :] = out[...].T


def after(values, done):
    return lax.optimization_barrier((values, done))[0]


def on_device(sources, leaf_ops, edge_slot, merge_ops, lift_ops, coupling, inverse, boundary):
    x, z, y, c = (lax.axis_index(axis) for axis in ("x", "z", "y", "c"))
    slot = edge_slot[0, 0]
    merge = merge_ops[0, 0]
    leaf = leaf_ops[0, 0]

    def part_of(value, bit, size):
        given = lax.dynamic_slice_in_dim(value, (1 - bit) * size, size, 0)
        return given, lax.dynamic_slice_in_dim(value, bit * size, size, 0)

    with jax.named_scope("reduction"):
        onehot = (slot[:, None] == jnp.arange(256, dtype=jnp.int32)[None, :]).astype(f32)
        merge_first = lax.dot_general(
            merge, onehot, (((1,), (0,)), ((), ())), precision=lax.Precision.HIGHEST, preferred_element_type=f32
        )
        given, kept = part_of(sources[0, 0], z >> 1, 256)
        given_on, given_kept = part_of(dot_t(given, leaf, None), z & 1, 128)
        given_on = dot_t(given_on, merge_first)
        given_kept = dot_t(given_kept, merge_first)

    with jax.named_scope("operators"):
        pieces = pl.pallas_call(
            cut_body,
            out_shape=[jax.ShapeDtypeStruct((64, 512), f32)] * 8,
            in_specs=[pl.BlockSpec(memory_space=pltpu.HBM)] * 2,
            scratch_shapes=[pltpu.VMEM((64, 2048), f32)] * 2 + [pltpu.SemaphoreType.DMA((2,))],
            compiler_params=pltpu.CompilerParams(vmem_limit_bytes=16 * 2**20),
        )(coupling[0], inverse[0])
        arrived = []
        for k in sent:
            arrived += [swap(pieces[k], "z", k) if k else pieces[0], swap(pieces[4 + k], "y", k) if k else pieces[4]]
        block = local_kernel(stack_body, [(2, 256, 512)])(*after(arrived, given_kept))[0]
        operators = lax.all_gather(block, ("x", "c"), axis=0)

    with jax.named_scope("reduction"):
        sent_on = swap(given_on, "z", 2)
        sent_kept = swap(given_kept, "z", 2)
        kept_on, kept_kept = part_of(dot_t(kept, leaf, None), z & 1, 128)
        kept_on = dot_t(kept_on, merge_first) + sent_on
        kept_kept = dot_t(kept_kept, merge_first) + sent_kept
        current = dot_t(kept_kept, merge) + swap(dot_t(kept_on, merge), "z", 1)
        given, kept = part_of(current, y >> 1, 64)
        level2 = dot_t(kept, merge) + swap(dot_t(given, merge), "y", 2)

    with jax.named_scope("boundary"):
        by_box = boundary.reshape(4, 4, 2, 16, 64)
        of_plane = lax.dynamic_index_in_dim(by_box, x, 1, keepdims=False)
        mine = lax.dynamic_index_in_dim(of_plane, c, 1, keepdims=False).reshape(64, 64)
        other = lax.dynamic_index_in_dim(of_plane, 1 - c, 1, keepdims=False).reshape(64, 64)
        theirs = swap(after(other, current), "c", 1)
        wide = jnp.concatenate([jnp.where(c == 0, mine, theirs), jnp.where(c == 0, theirs, mine)], axis=1)
        entering_parts = exchange([after(wide, level2)] * 4, "y")

    with jax.named_scope("reduction"):
        given, kept = part_of(level2, y & 1, 32)
        level3 = dot_t(kept, merge) + swap(dot_t(given, merge), "y", 1)
        given, kept = part_of(level3, c, 16)
        current = dot_t(kept, merge) + swap(dot_t(given, merge), "c", 1)

    with jax.named_scope("boundary"):
        entering = local_kernel(widen_body, [(64, 512)], scratch=[(4, 64, 128)])(*entering_parts)[0]

    with jax.named_scope("loads"):
        l_pieces = local_kernel(lift_body, [(16, 512)] * 4, 3 * 2 * 16 * 256 * 2048, 2**21, [(16, 2048)])(
            current, lift_ops[0, 0]
        )
        arrived = []
        for k in range(4):
            pairs = [(s * 4 + y0, y0 * 4 + (s + k) % 4) for s in range(4) for y0 in range(4)]
            arrived.append(lax.ppermute(l_pieces[k], ("x", "y"), pairs))
        loads = [select(arrived, (y - s) % 4) for s in range(4)]

    with jax.named_scope("chain"):
        solutions = []
        flops = 3 * 2 * 64 * 512 * 512
        parts = [entering]
        for s in range(4):
            out_shapes = [(64, 512)] + ([(64, 128)] if s else [])
            couple = local_kernel(
                functools.partial(couple_body, len(parts)), out_shapes, flops, 2**21, [(64, 512)] if s else []
            )
            of_slab = after(operators, partial) if s else operators
            results = couple(*parts, loads[s], of_slab[2 * s, 0], of_slab[2 * s + 1, 0])
            solutions += results[1:]
            partial = results[0]
            parts = exchange([partial] * 4, "z")
            invert = local_kernel(
                functools.partial(invert_body, s == 3),
                [(64, 512)] + ([(64, 128)] * 4 if s == 3 else []),
                flops,
                2**21,
            )
            of_slab = after(operators, partial)
            results = invert(*parts, of_slab[2 * s, 1], of_slab[2 * s + 1, 1])
            partial = results[0]
            if s < 3:
                parts = exchange([partial] * 4, "y")
            else:
                parts = exchange(results[1:], "y")
                solutions.append((parts[0] + parts[1]) + (parts[2] + parts[3]))

    with jax.named_scope("output"):
        parts = exchange([select(solutions, x ^ k) for k in range(4)], "x")
        theirs = swap(jnp.stack(parts), "c", 1)
        turned = local_kernel(finish_body, [(1, 64, 512)], scratch=[(512, 64)])(*parts, theirs)[0]
        return turned.transpose(0, 2, 1)


def solution(mesh):
    wide = Mesh(mesh.devices.reshape(4, 4, 4, 2), ("x", "z", "y", "c"))
    box = ("z", "y", "c")
    return jax.shard_map(
        on_device,
        mesh=wide,
        in_specs=(
            P("x", box, None, None),
            P("x", box, None, None),
            P("x", box, None),
            P("x", box, None, None),
            P("x", box, None, None),
            P("x", box, None),
            P("x", box, None),
            P(None, box),
        ),
        out_specs=P("x", None, box),
        check_vma=False,
    )
```

```python
import functools

import jax
import jax.numpy as jnp
from jax import lax
from jax.experimental import pallas as pl
from jax.experimental.pallas import tpu as pltpu
from jax.sharding import Mesh, PartitionSpec as P

contract_last = (((1,), (1,)), ((), ()))
f32 = jnp.float32
bf16 = jnp.bfloat16
sent = (0, 3, 2, 1)


def dot_t(a, b, precision=lax.Precision.HIGH):
    return lax.dot_general(a, b, contract_last, precision=precision, preferred_element_type=f32)


def swap(value, axis, mask):
    count = 2 if axis == "c" else 4
    return lax.ppermute(value, axis, [(i, i ^ mask) for i in range(count)])


def exchange(pieces, axis):
    return [pieces[0]] + [swap(pieces[k], axis, k) for k in sent[1:]]


def select(choices, index):
    chosen = choices[0]
    for k in range(1, len(choices)):
        chosen = jnp.where(index == k, choices[k], chosen)
    return chosen


def local_kernel(body, out_shapes, flops=0, bytes_accessed=2**20, scratch=()):
    return pl.pallas_call(
        body,
        out_shape=[jax.ShapeDtypeStruct(shape, f32) for shape in out_shapes],
        scratch_shapes=[pltpu.VMEM(shape, f32) for shape in scratch],
        cost_estimate=pl.CostEstimate(flops=flops, bytes_accessed=bytes_accessed, transcendentals=0),
        compiler_params=pltpu.CompilerParams(vmem_limit_bytes=16 * 2**20),
    )


def lanes(start, size=128):
    return pl.ds(pl.multiple_of(start, 128), size)


def rows(start, size):
    return pl.ds(pl.multiple_of(start, 16), size)


def place_columns(out, j, part):
    out[:, j * 64 : j * 64 + 64] = part[:, :64]
    out[:, 256 + j * 64 : 256 + j * 64 + 64] = part[:, 64:]


def cut_body(c_ref, i_ref, *outs):
    z, y = lax.axis_index("z"), lax.axis_index("y")
    for k in range(4):
        for j in range(4):
            place_columns(outs[k], j, c_ref[:, lanes((z ^ k) * 512 + j * 128)])
            place_columns(outs[4 + k], j, i_ref[:, lanes(j * 512 + (y ^ k) * 128)])


def stack_body(*refs):
    z, y = lax.axis_index("z"), lax.axis_index("y")
    block = refs[8]
    for i, k in enumerate(sent):
        block[0, rows((z ^ k) * 64, 64), :] = refs[2 * i][...]
        block[1, rows((y ^ k) * 64, 64), :] = refs[2 * i + 1][...]


def widen_body(a0, a1, a2, a3, out, scratch):
    y = lax.axis_index("y")
    for k, part in zip(sent, (a0, a1, a2, a3)):
        scratch[y ^ k] = part[...]
    for j in range(4):
        place_columns(out, j, scratch[j])


def split(value):
    high = value.astype(bf16)
    return high, (value - high.astype(f32)).astype(bf16)


def product(value, operator):
    def dot(a, b):
        return lax.dot_general(a, b, contract_last, preferred_element_type=f32)

    vh, vl = split(value)
    oh, ol = split(operator)
    return dot(vh, oh) + (dot(vh, ol) + dot(vl, oh))


def natural_columns(ref, y):
    parts = []
    for core in range(2):
        wide = ref[:, lanes(core * 256 + lax.shift_right_logical(y, 1) * 128)]
        parts.append(jnp.where((y & 1) == 0, wide[:, :64], wide[:, 64:]))
    return jnp.concatenate(parts, axis=1)


def add_up(refs):
    total = refs[0][...]
    for ref in refs[1:]:
        total = total + ref[...]
    return total


def couple_body(n_parts, *refs):
    parts, (load, w0, w1), outs = refs[:n_parts], refs[n_parts : n_parts + 3], refs[n_parts + 3 :]
    out = outs[0]
    entering = add_up(parts)
    if n_parts > 1:
        total = outs[2]
        total[...] = entering
        outs[1][...] = natural_columns(total, lax.axis_index("y"))
    out[:, :256] = -product(entering, w0[...])
    out[:, 256:] = -product(entering, w1[...])
    own = rows(lax.axis_index("z") * 16, 16)
    out[own, :] = out[own, :] + load[...]


def invert_body(last, a0, a1, a2, a3, w0, w1, out, *pieces):
    corrected = add_up((a0, a1, a2, a3))
    out[:, :256] = product(corrected, w0[...])
    out[:, 256:] = product(corrected, w1[...])
    if last:
        y = lax.axis_index("y")
        for k, piece in enumerate(pieces):
            piece[...] = natural_columns(out, y ^ k)


def lift_body(current, lift, *refs):
    outs, lifted = refs[:4], refs[4]
    x = lax.axis_index("x")
    for j in range(4):
        lifted[:, j * 512 : (j + 1) * 512] = product(current[...], lift[j * 512 : (j + 1) * 512, :])
    for k, out in enumerate(outs):
        to = lax.rem(x + k, 4)
        for j in range(4):
            place_columns(out, j, lifted[:, lanes(j * 512 + to * 128)])


def finish_body(a0, a1, a2, a3, theirs, turned, out):
    x, c = lax.axis_index("x"), lax.axis_index("c")
    for i, part in enumerate((a0, a1, a2, a3)):
        k = sent[i]
        for z0 in range(4):
            mine = part[z0 * 16 : z0 * 16 + 16, :]
            other = theirs[i, z0 * 16 : z0 * 16 + 16, :]
            base = z0 * 128 + (x ^ k) * 32
            out[rows(base + c * 16, 16), :] = jnp.where(c == 0, mine[:, :64], mine[:, 64:])
            out[rows(base + (1 - c) * 16, 16), :] = jnp.where(c == 0, other[:, :64], other[:, 64:])
    turned[0, :, :] = out[...].T


def after(values, done):
    return lax.optimization_barrier((values, done))[0]


def on_device(sources, leaf_ops, edge_slot, merge_ops, lift_ops, coupling, inverse, boundary):
    x, z, y, c = (lax.axis_index(axis) for axis in ("x", "z", "y", "c"))
    slot = edge_slot[0, 0]
    merge = merge_ops[0, 0]
    leaf = leaf_ops[0, 0]

    def part_of(value, bit, size):
        given = lax.dynamic_slice_in_dim(value, (1 - bit) * size, size, 0)
        return given, lax.dynamic_slice_in_dim(value, bit * size, size, 0)

    with jax.named_scope("reduction"):
        onehot = (slot[:, None] == jnp.arange(256, dtype=jnp.int32)[None, :]).astype(f32)
        merge_first = lax.dot_general(
            merge, onehot, (((1,), (0,)), ((), ())), precision=lax.Precision.HIGHEST, preferred_element_type=f32
        )
        given, kept = part_of(sources[0, 0], z >> 1, 256)
        given_on, given_kept = part_of(dot_t(given, leaf, None), z & 1, 128)
        given_on = dot_t(given_on, merge_first)
        given_kept = dot_t(given_kept, merge_first)

    with jax.named_scope("operators"):
        pieces = local_kernel(cut_body, [(64, 512)] * 8)(coupling[0], inverse[0])
        arrived = []
        for k in sent:
            arrived += [swap(pieces[k], "z", k) if k else pieces[0], swap(pieces[4 + k], "y", k) if k else pieces[4]]
        block = local_kernel(stack_body, [(2, 256, 512)])(*arrived)[0]
        operators = lax.all_gather(block, ("x", "c"), axis=0)

    with jax.named_scope("reduction"):
        sent_on = swap(given_on, "z", 2)
        sent_kept = swap(given_kept, "z", 2)
        kept_on, kept_kept = part_of(dot_t(kept, leaf, None), z & 1, 128)
        kept_on = dot_t(kept_on, merge_first) + sent_on
        kept_kept = dot_t(kept_kept, merge_first) + sent_kept
        current = dot_t(kept_kept, merge) + swap(dot_t(kept_on, merge), "z", 1)
        given, kept = part_of(current, y >> 1, 64)
        level2 = dot_t(kept, merge) + swap(dot_t(given, merge), "y", 2)

    with jax.named_scope("boundary"):
        by_box = boundary.reshape(4, 4, 2, 16, 64)
        of_plane = lax.dynamic_index_in_dim(by_box, x, 1, keepdims=False)
        mine = lax.dynamic_index_in_dim(of_plane, c, 1, keepdims=False).reshape(64, 64)
        other = lax.dynamic_index_in_dim(of_plane, 1 - c, 1, keepdims=False).reshape(64, 64)
        theirs = swap(after(other, current), "c", 1)
        wide = jnp.concatenate([jnp.where(c == 0, mine, theirs), jnp.where(c == 0, theirs, mine)], axis=1)
        entering_parts = exchange([after(wide, level2)] * 4, "y")

    with jax.named_scope("reduction"):
        given, kept = part_of(level2, y & 1, 32)
        level3 = dot_t(kept, merge) + swap(dot_t(given, merge), "y", 1)
        given, kept = part_of(level3, c, 16)
        current = dot_t(kept, merge) + swap(dot_t(given, merge), "c", 1)

    with jax.named_scope("boundary"):
        entering = local_kernel(widen_body, [(64, 512)], scratch=[(4, 64, 128)])(*entering_parts)[0]

    with jax.named_scope("loads"):
        l_pieces = local_kernel(lift_body, [(16, 512)] * 4, 3 * 2 * 16 * 256 * 2048, 2**21, [(16, 2048)])(
            current, lift_ops[0, 0]
        )
        arrived = []
        for k in range(4):
            pairs = [(s * 4 + y0, y0 * 4 + (s + k) % 4) for s in range(4) for y0 in range(4)]
            arrived.append(lax.ppermute(l_pieces[k], ("x", "y"), pairs))
        loads = [select(arrived, (y - s) % 4) for s in range(4)]

    with jax.named_scope("chain"):
        solutions = []
        flops = 3 * 2 * 64 * 512 * 512
        parts = [entering]
        for s in range(4):
            out_shapes = [(64, 512)] + ([(64, 128)] if s else [])
            couple = local_kernel(
                functools.partial(couple_body, len(parts)), out_shapes, flops, 2**21, [(64, 512)] if s else []
            )
            of_slab = after(operators, partial) if s else operators
            results = couple(*parts, loads[s], of_slab[2 * s, 0], of_slab[2 * s + 1, 0])
            solutions += results[1:]
            partial = results[0]
            parts = exchange([partial] * 4, "z")
            invert = local_kernel(
                functools.partial(invert_body, s == 3),
                [(64, 512)] + ([(64, 128)] * 4 if s == 3 else []),
                flops,
                2**21,
            )
            of_slab = after(operators, partial)
            results = invert(*parts, of_slab[2 * s, 1], of_slab[2 * s + 1, 1])
            partial = results[0]
            if s < 3:
                parts = exchange([partial] * 4, "y")
            else:
                parts = exchange(results[1:], "y")
                solutions.append((parts[0] + parts[1]) + (parts[2] + parts[3]))

    with jax.named_scope("output"):
        parts = exchange([select(solutions, x ^ k) for k in range(4)], "x")
        theirs = swap(jnp.stack(parts), "c", 1)
        turned = local_kernel(finish_body, [(1, 64, 512)], scratch=[(512, 64)])(*parts, theirs)[0]
        return turned.transpose(0, 2, 1)


def solution(mesh):
    wide = Mesh(mesh.devices.reshape(4, 4, 4, 2), ("x", "z", "y", "c"))
    box = ("z", "y", "c")
    return jax.shard_map(
        on_device,
        mesh=wide,
        in_specs=(
            P("x", box, None, None),
            P("x", box, None, None),
            P("x", box, None),
            P("x", box, None, None),
            P("x", box, None, None),
            P("x", box, None),
            P("x", box, None),
            P(None, box),
        ),
        out_specs=P("x", None, box),
        check_vma=False,
    )
```
